512 devices in a mesh: pipe: 4 (over y_lo), dp: 64 (over z, x, core), param: 2 (over y_hi).
Axes of the slice: x: 4, y: 8 (y_hi: 2, y_lo: 4; y = y_hi * 4 + y_lo), z: 8, core: 2. Of those that a mesh axis runs over, the one named last changes fastest.
Arguments:
- hidden: bfloat16 [4, 32768, 1920], P('pipe', 'dp'), may hold values from -16 to 16
- targets: bfloat16 [4, 32768, 1024], P('pipe', 'dp', 'param'), may hold values from -0.1875 to 0.1875
- w_proj: bfloat16 [1920, 1024], P('dp', 'param'), may hold values from -0.125 to 0.125
- mask_counts: int32 [4, 64], P('pipe', 'dp'), may hold values from 32 to 256, as said below
- mask_pos: int32 [4, 64, 256], P('pipe', 'dp'), may hold values from 0 to 32767, as said below
- negatives: int32 [4, 64, 100, 256], P('pipe', 'dp'), may hold values from 0 to 32767, as said below
Outputs:
- grad_w: float32 [1920, 1024], P('dp', 'param')
- upstream: bfloat16 [4, 32768, 1920], P('pipe', 'dp', 'param')
- grad_targets: bfloat16 [4, 32768, 1024], P('pipe', 'dp', 'param')
The draws below stay inside these ranges and needn't reach their ends.
Inputs may be any that keep to these rules, and one draw needn't show every extreme that they name: In every micro-batch some data shard has all 256 slots live; the first mask_counts slots of a shard are live, the others are ignored. `mask_pos`: the 256 slots of data shard j name distinct frames of that shard, j * 512 to (j + 1) * 512 - 1. `negatives`: distractors of a slot are frames of the same utterance as the slot's frame, never that frame, possibly repeated; each lies in the slot's data shard or an adjacent one.
All inputs are finite; a program needn't handle non-finite values.
Results may differ from the reference program's by a relative error of at most 0.0065.
Values may be sent and summed in bfloat16 or wider, within the bound.
No kernel may reach another device: no remote copies, remote signals or barrier semaphores. Data moves between devices by JAX's collectives and lax.ppermute only.
A program may use at most 64 MiB of HBM per device.

```python
import jax
import jax.numpy as jnp
from jax import lax

D = 1920
E = 1024
NEG = 100
T_DEV = 512
M_CAP = 256
MICRO = 4
FRAMES = 32768
N_PIPE = 4
N_DP = 64


def utterance_frames(key):
    shortest = T_DEV // 4
    count = FRAMES // shortest + 1
    lengths = jax.random.randint(jax.random.fold_in(key, 11), (MICRO, count), shortest, 3 * T_DEV // 4 + 1)
    ends = jnp.cumsum(lengths, axis=1)
    starts = jnp.concatenate([jnp.zeros((MICRO, 1), jnp.int32), ends[:, :-1].astype(jnp.int32)], axis=1)
    starts = jnp.where((starts == 0) | (starts <= FRAMES - shortest), starts, FRAMES)
    shards = FRAMES // T_DEV
    keys = jax.random.split(jax.random.fold_in(key, 12), MICRO * shards)

    def pick_slots(single):
        return jax.random.permutation(single, T_DEV)[:M_CAP].astype(jnp.int32)
    local = jax.vmap(pick_slots)(keys).reshape(MICRO, shards, M_CAP)
    offsets = (jnp.arange(shards, dtype=jnp.int32) * T_DEV)[None, :, None]
    return (starts, local + offsets)


def draw_mask_pos(key, part):
    starts, positions = utterance_frames(key)
    return positions.astype(jnp.int32)


def draw_negatives(key, part):
    starts, positions = utterance_frames(key)
    key = jax.random.fold_in(key, 3)
    shards = FRAMES // T_DEV
    flat = positions.reshape(MICRO, shards * M_CAP)
    below = starts[:, None, :] <= flat[:, :, None]
    begin = jnp.max(jnp.where(below, starts[:, None, :], 0), axis=2)
    finish = jnp.min(jnp.where(below, FRAMES, starts[:, None, :]), axis=2)
    span = finish - begin
    offset = jax.random.randint(key, (MICRO, NEG, shards * M_CAP), 0, span[:, None, :] - 1)
    chosen = begin[:, None, :] + offset
    chosen = chosen + (chosen >= flat[:, None, :]).astype(jnp.int32)
    chosen = chosen.reshape(MICRO, NEG, shards, M_CAP)
    return jnp.transpose(chosen, (0, 2, 1, 3)).astype(jnp.int32)


def draw_mask_counts(key, part):
    key = jax.random.fold_in(key, 5)
    shards = FRAMES // T_DEV
    lowest = max(1, M_CAP // 8)
    counts = jax.random.randint(key, (MICRO, shards), lowest, M_CAP + 1)
    fullest = jax.random.randint(jax.random.fold_in(key, 1), (MICRO,), 0, shards)
    where_full = jnp.arange(shards, dtype=jnp.int32)[None, :] == fullest[:, None]
    return jnp.where(where_full, M_CAP, counts).astype(jnp.int32)


def spiked(values, rng, source, target, parts, factor):
    owner, partner = [(jnp.arange(values.shape[axis_at]) // (values.shape[axis_at] // parts)).reshape([-1 if axis == axis_at else 1 for axis in range(values.ndim)]) for axis_at in (source, target)]
    chosen = jax.random.permutation(rng, parts)[partner]
    strong = (owner == chosen) | (owner == (partner + parts // 2) % parts)
    return jnp.where(strong, factor * values, values)


def level_of(key, dims, cuts, low, high):
    def one(dim, shards_of):
        heights = jax.random.uniform(jax.random.fold_in(jax.random.fold_in(key, 6), dim), (shards_of,), jnp.float32, low / len(cuts), high / len(cuts))
        return jnp.repeat(jnp.exp(heights), dims[dim] // shards_of).reshape((-1,) + (1,) * (len(dims) - dim - 1))

    level = one(*cuts[0])
    for cut in cuts[1:]:
        level = level * one(*cut)
    return level


def noise(key, extent, scale, bound, cuts=(), held_as=jnp.bfloat16):
    result = jax.random.normal(key, extent, jnp.float32) * scale
    if len(cuts) > 0:
        result = level_of(key, extent, cuts, -0.22, 0.18) * result
    return jnp.clip(result, min=-bound, max=bound).astype(held_as)


def noise_with(key, extent, scale, limit, pieces, heavy, kind=jnp.bfloat16):
    array = scale * jax.random.normal(key, extent, jnp.float32)
    if pieces:
        array = array * level_of(key, extent, pieces, -0.22, 0.18)
    return jnp.clip(spiked(array, jax.random.fold_in(key, 3), *heavy), -limit, limit).astype(kind)


def setup_inputs(seed: int = 0) -> dict:
    splits = jax.random.split(jax.random.key(seed), 7)
    hidden = noise_with(splits[0], (MICRO, FRAMES, D), 1.0, 16.0, ((0, 4), (1, 64)), (1, 2, 64, 4.0))
    targets = noise(splits[1], (MICRO, FRAMES, E), 0.03125, 0.1875, ((0, 4), (1, 64), (2, 2)))
    w_proj = noise(splits[2], (D, E), D ** -0.5, 0.125, ((0, 64), (1, 2)))
    mask_counts = draw_mask_counts(jax.random.fold_in(splits[6], 71), 0)
    mask_pos = draw_mask_pos(jax.random.fold_in(splits[6], 71), 0)
    negatives = draw_negatives(jax.random.fold_in(splits[6], 71), 0)
    return {"hidden": hidden, "targets": targets, "w_proj": w_proj, "mask_counts": mask_counts, "mask_pos": mask_pos, "negatives": negatives}


sharpness_divisor = 0.1
loss_multiplier = 32.0
epsilon = 1e-06

def shard_backward(carry, inputs, frames_here, padded_units, w_proj, width):
    grad_w, grad_pad = carry
    shard_index, live_count, positions, distract = inputs
    rows = jnp.take(frames_here, positions, axis=0)
    context = jnp.dot(rows, w_proj, preferred_element_type=jnp.float32)
    inverse = 1.0 / jnp.sqrt(lax.optimization_barrier(jnp.sum(context * context, axis=1)) + epsilon)
    ctx_unit = (context * inverse[:, None]).astype(jnp.bfloat16)
    window = lax.dynamic_slice_in_dim(padded_units, shard_index * width, 3 * width, 0)
    similarity_table = jnp.dot(ctx_unit, window.T, preferred_element_type=jnp.float32)
    candidate_similarity_entries = (jnp.concatenate([positions[None, :], distract], axis=0) - (shard_index - 1) * width).T
    unnormalized_table = jnp.take_along_axis(similarity_table, candidate_similarity_entries, axis=1) / sharpness_divisor
    expon = jnp.exp(unnormalized_table)
    normalized_probabilities = expon / lax.optimization_barrier(jnp.sum(expon, axis=1, keepdims=True))
    slot_ids = jnp.arange(positions.shape[0], dtype=jnp.int32)
    usable_flags = (slot_ids < live_count).astype(jnp.float32)
    first_position = (jnp.arange(candidate_similarity_entries.shape[1], dtype=jnp.int32) == 0).astype(jnp.float32)
    unnormalized_derivative = loss_multiplier * usable_flags[:, None] * (normalized_probabilities - first_position[None, :]) / sharpness_divisor
    dscore = jnp.zeros(similarity_table.shape, jnp.float32).at[slot_ids[:, None], candidate_similarity_entries].add(unnormalized_derivative)
    dscore = dscore.astype(jnp.bfloat16)
    dunit = jnp.dot(dscore, window, preferred_element_type=jnp.float32)
    dwindow = jnp.dot(dscore.T, ctx_unit, preferred_element_type=jnp.float32)
    along = lax.optimization_barrier(jnp.sum(context * dunit, axis=1))
    dctx = (dunit * inverse[:, None] - context * (along * inverse ** 3)[:, None]).astype(jnp.bfloat16)
    grad_w = grad_w + jnp.dot(rows.T, dctx, preferred_element_type=jnp.float32)
    drows = jnp.dot(dctx, w_proj.T, preferred_element_type=jnp.float32).astype(jnp.bfloat16)
    begin = shard_index * width
    current = lax.dynamic_slice_in_dim(grad_pad, begin, 3 * width, 0)
    grad_pad = lax.dynamic_update_slice_in_dim(grad_pad, current + dwindow, begin, 0)
    return ((grad_w, grad_pad), drows)

def reference(hidden, targets, w_proj, mask_counts, mask_pos, negatives):
    width = T_DEV
    grad_w = jnp.zeros(w_proj.shape, jnp.float32)
    uppers = []
    target_grads = []
    for section in range(N_PIPE):
        frames_here = hidden[section]
        target_f = targets[section].astype(jnp.float32)
        inv_tgt = 1.0 / jnp.sqrt(lax.optimization_barrier(jnp.sum(target_f * target_f, axis=1)) + epsilon)
        tgt_unit = (target_f * inv_tgt[:, None]).astype(jnp.bfloat16)
        padded = jnp.pad(tgt_unit, ((width, width), (0, 0)))
        grad_pad = jnp.zeros((FRAMES + 2 * width, E), jnp.float32)

        def step_fn(carry, inputs):
            return shard_backward(carry, inputs, frames_here, padded, w_proj, width)
        inputs = (jnp.arange(N_DP, dtype=jnp.int32), mask_counts[section], mask_pos[section], negatives[section])
        (grad_w, grad_pad), drows = lax.scan(step_fn, (grad_w, grad_pad), inputs)
        dtgt_unit = grad_pad[width:width + FRAMES]
        along_t = lax.optimization_barrier(jnp.sum(target_f * dtgt_unit, axis=1))
        grad_t = dtgt_unit * inv_tgt[:, None] - target_f * (along_t * inv_tgt ** 3)[:, None]
        target_grads.append(grad_t.astype(jnp.bfloat16))
        dhidden = jnp.zeros((FRAMES, D), jnp.bfloat16).at[mask_pos[section].reshape(-1)].set(drows.reshape(-1, D))
        uppers.append(dhidden)
    upstream = jnp.stack(uppers[1:] + uppers[:1])
    return (grad_w, upstream, jnp.stack(target_grads))
```

```python
import jax
import jax.numpy as jnp
from jax import lax
from jax.experimental import pallas as pl
from jax.experimental.pallas import tpu as pltpu
from jax.sharding import PartitionSpec as P

sharpness_divisor = 0.1
loss_multiplier = 32.0
epsilon = 1e-06

F32 = jnp.float32
BF16 = jnp.bfloat16
I32 = jnp.int32

LANES = 128
SLOTS = 256
FRAMES = 512
WINDOW = 3 * FRAMES
TILES = WINDOW // LANES
COLUMNS = 101
SPARE = LANES - 1
MODEL = 1920
FEATS = 512
BLOCK = 30
PAD = 32
PEERS = 32
HALF = PEERS * PAD


def iota(shape, dim):
    return lax.broadcasted_iota(I32, shape, dim)


def one_hot(hits):
    return jnp.where(hits, 1.0, 0.0).astype(BF16)


def dot(left, right):
    return jnp.dot(left, right, preferred_element_type=F32)


def dot_cols(left, right):
    return lax.dot_general(left, right, (((1,), (1,)), ((), ())), preferred_element_type=F32)


def dot_rows(left, right):
    return lax.dot_general(left, right, (((0,), (0,)), ((), ())), preferred_element_type=F32)


def lookup(table, index):
    return jnp.take_along_axis(table, index, axis=1, mode="promise_in_bounds")


def call(body, outs, n_scalars, n_arrays, scratch=(), flops=0, bytes_accessed=0):
    return pl.pallas_call(
        body,
        out_shape=tuple(jax.ShapeDtypeStruct(shape, dtype) for shape, dtype in outs),
        in_specs=[pl.BlockSpec(memory_space=pltpu.SMEM)] * n_scalars
        + [pl.BlockSpec(memory_space=pltpu.VMEM)] * n_arrays,
        out_specs=tuple(pl.BlockSpec(memory_space=pltpu.VMEM) for _ in outs),
        scratch_shapes=list(scratch),
        compiler_params=pltpu.CompilerParams(vmem_limit_bytes=32 * 1024 * 1024),
        cost_estimate=pl.CostEstimate(
            flops=flops, bytes_accessed=bytes_accessed, transcendentals=0
        ),
    )


def rows_body(core_ref, pos_ref, hidden_ref, own_ref, other_ref, own_t_ref, other_t_ref):
    chosen = one_hot(pos_ref[...] == iota((SLOTS, FRAMES), 1))
    rows = dot(chosen, hidden_ref[...]).astype(BF16)
    core = core_ref[0]
    step = 256
    for parity, straight, turned in ((core, own_ref, own_t_ref), (1 - core, other_ref, other_t_ref)):
        for k in range(HALF // step):
            low = (2 * BLOCK * step // PAD * k) // LANES * LANES
            wide = min(MODEL, low + 640) - low
            piece = rows[:, low : low + wide]
            q = iota((step, wide), 0) + step * k
            wanted = BLOCK * (2 * (q >> 5) + parity) + (q & 31)
            spread = one_hot((wanted == iota((step, wide), 1) + low) & ((q & 31) < BLOCK))
            straight[:, step * k : step * (k + 1)] = dot_cols(piece, spread).astype(BF16)
            turned[step * k : step * (k + 1), :] = dot_cols(spread, piece).astype(BF16)


def index_body(frame_ref, column_ref, times_ref):
    lane = iota((8, LANES), 1)
    tiles = [lane + LANES * t for t in range(TILES)]

    def group(g, carry):
        rows = pl.ds(pl.multiple_of(g * 8, 8), 8)
        frame = frame_ref[rows, :]
        found = [jnp.full((8, LANES), SPARE, I32) for _ in range(TILES)]
        times = jnp.zeros((8, LANES), F32)
        for c in range(COLUMNS):
            this = jnp.broadcast_to(frame[:, c : c + 1], (8, LANES))
            times = times + jnp.where(frame == this, 1.0, 0.0)
            for t in range(TILES):
                found[t] = jnp.where(this == tiles[t], c, found[t])
        for t in range(TILES):
            column_ref[rows, LANES * t : LANES * (t + 1)] = found[t]
        times_ref[rows, :] = times
        return carry

    lax.fori_loop(0, SLOTS // 8, group, 0)


def score_body(own_ref, other_ref, w_own_ref, w_other_ref, window_ref, frame_ref, norm_ref, sent_ref, context_ref, table_ref):
    context = dot(own_ref[...], w_own_ref[...]) + dot(other_ref[...], w_other_ref[...])
    context_ref[...] = context
    table_ref[...] = dot_cols(context.astype(BF16), window_ref[...])
    sent_ref[0:SLOTS, :] = jnp.broadcast_to(
        jnp.sum(context * context, axis=1, keepdims=True), (SLOTS, LANES)
    )
    sent_ref[SLOTS : SLOTS + 16, :] = norm_ref[...]
    lane = iota((16, LANES), 1)

    def group(g, carry):
        rows = pl.ds(pl.multiple_of(g * 16, 16), 16)
        frame = frame_ref[rows, :]
        tile, place = frame >> 7, frame & 127
        picked = jnp.where(lane == COLUMNS, sent_ref[rows, :], 0.0)
        for t in range(TILES):
            found = lookup(table_ref[rows, LANES * t : LANES * (t + 1)], place)
            picked = jnp.where((tile == t) & (lane < COLUMNS), found, picked)
        sent_ref[rows, :] = picked
        return carry

    lax.fori_loop(0, SLOTS // 16, group, 0)


def slots_body(
    count_ref, sent_ref, got_ref, context_ref, frame_ref, times_ref, column_ref, window_ref,
    dctx_ref, unit_ref, step_ref, along_ref, inverse_ref, shift_ref, scores_ref,
):
    inv_tgt = 1.0 / jnp.sqrt(
        sent_ref[SLOTS : SLOTS + 16, :] + got_ref[SLOTS : SLOTS + 16, :] + epsilon
    )
    lane = iota((16, LANES), 1)
    named = lane < COLUMNS
    count = count_ref[0]

    def group(g, carry):
        rows = pl.ds(pl.multiple_of(g * 16, 16), 16)
        raw = sent_ref[rows, :] + got_ref[rows, :]
        inverse = 1.0 / jnp.sqrt(raw[:, COLUMNS : COLUMNS + 1] + epsilon)
        frame = frame_ref[rows, :]
        tile, place = frame >> 7, frame & 127
        scale = jnp.zeros((16, LANES), F32)
        for t in range(TILES):
            line = jnp.broadcast_to(inv_tgt[t : t + 1, :], (16, LANES))
            scale = jnp.where(tile == t, lookup(line, place), scale)
        logits = raw * inverse * scale / sharpness_divisor
        expon = jnp.where(named, jnp.exp(jnp.where(named, logits, 0.0)), 0.0)
        probs = expon / jnp.sum(expon, axis=1, keepdims=True)
        live = iota((16, LANES), 0) + g * 16 < count
        first = jnp.where(lane == 0, 1.0, 0.0)
        step = jnp.where(live & named, loss_multiplier * (probs - first) / sharpness_divisor, 0.0)
        times = jnp.maximum(times_ref[rows, :], 1.0)
        step = step * times
        weight = (step * scale).astype(BF16).astype(F32)
        along = jnp.sum(jnp.where(named, weight * raw / times, 0.0), axis=1, keepdims=True)
        step_ref[rows, :] = step
        along_ref[rows, :] = jnp.where(named, step.astype(BF16).astype(F32) * raw * inverse, 0.0)
        inverse_ref[rows, :] = jnp.broadcast_to(inverse, (16, LANES))
        shift_ref[rows, :] = jnp.broadcast_to(along * inverse * inverse * inverse, (16, LANES))
        for t in range(TILES):
            span = slice(LANES * t, LANES * (t + 1))
            scores_ref[rows, span] = lookup(weight, column_ref[rows, span]).astype(BF16)
        return carry

    lax.fori_loop(0, SLOTS // 16, group, 0)
    context = context_ref[...]
    inverse = inverse_ref[:, 0:1]
    dunit = dot(scores_ref[...], window_ref[...])
    dctx_ref[...] = (dunit * inverse - context * shift_ref[:, 0:1]).astype(BF16)
    unit_ref[...] = (context * inverse).astype(BF16)


def frames_body(step_ref, along_ref, column_ref, unit_ref, low_ref, own_ref, high_ref, line_ref, scores_ref, sums_ref):
    sums_ref[...] = jnp.zeros((16, WINDOW), F32)

    def group(g, carry):
        rows = pl.ds(pl.multiple_of(g * 16, 16), 16)
        step = step_ref[rows, :]
        along = along_ref[rows, :]
        for t in range(TILES):
            span = slice(LANES * t, LANES * (t + 1))
            index = column_ref[rows, span]
            scores_ref[rows, span] = lookup(step, index).astype(BF16)
            sums_ref[:, span] += lookup(along, index)
        return carry

    lax.fori_loop(0, SLOTS // 16, group, 0)
    line = jnp.sum(sums_ref[...], axis=0, keepdims=True)
    line_ref[...] = jnp.broadcast_to(line[:, FRAMES : 2 * FRAMES], (8, FRAMES))
    row = iota((16, FRAMES), 0)
    for part, ref in ((0, low_ref), (1, own_ref), (2, high_ref)):
        span = slice(FRAMES * part, FRAMES * (part + 1))
        ref[0:FRAMES, :] = dot_rows(scores_ref[:, span], unit_ref[...]).astype(ref.dtype)
        if part != 1:
            left = jnp.broadcast_to(line[:, span], (16, FRAMES))
            first = left.astype(BF16).astype(F32)
            second = (left - first).astype(BF16).astype(F32)
            third = left - first - second
            ref[FRAMES : FRAMES + 16, :] = jnp.where(
                row == 0, first, jnp.where(row == 1, second, jnp.where(row == 2, third, 0.0))
            ).astype(BF16)


def drows_body(half_ref, dctx_ref, w_own_ref, w_other_ref, same_ref, cross_ref):
    half = half_ref[0]
    dctx = dctx_ref[...]
    for ref, which in ((same_ref, half), (cross_ref, 1 - half)):
        rows = pl.ds(pl.multiple_of(which * (HALF // 2), HALF // 2), HALF // 2)
        ref[:, 0 : HALF // 2] = dot_cols(dctx, w_own_ref[rows, :]).astype(BF16)
        ref[:, HALF // 2 : HALF] = dot_cols(dctx, w_other_ref[rows, :]).astype(BF16)


def spread_body(core_ref, pos_ref, same_ref, cross_ref, out_ref):
    core = core_ref[0]
    drows = (same_ref[...].astype(F32) + cross_ref[...].astype(F32)).astype(BF16)
    q = iota((HALF, MODEL // 2), 0)
    parity = jnp.where(q < HALF // 2, core, 1 - core)
    wanted = BLOCK * (2 * ((q >> 5) & 15) + parity) + (q & 31)
    unpad = one_hot((wanted == iota((HALF, MODEL // 2), 1)) & ((q & 31) < BLOCK))
    rows = dot(drows, unpad).astype(BF16)
    placed = one_hot(iota((FRAMES, SLOTS), 0) == pos_ref[...])
    out_ref[...] = dot(placed, rows).astype(BF16)


def local(hidden, targets, w_proj, mask_counts, mask_pos, negatives):
    shard = lax.axis_index("dp")
    core = (shard % 2).astype(I32).reshape(1)
    half = lax.axis_index("param").astype(I32).reshape(1)
    n_dp = lax.axis_size("dp")
    n_pipe = lax.axis_size("pipe")
    peers = [[2 * i + c for i in range(n_dp // 2)] for c in range(2)]
    swap = [(i, i ^ 1) for i in range(n_dp)]
    upward = [(i, i + 1) for i in range(n_dp - 1)]
    downward = [(i + 1, i) for i in range(n_dp - 1)]
    back = [(i, (i - 1) % n_pipe) for i in range(n_pipe)]
    back_across = [
        (2 * i + a, 2 * ((i - 1) % n_pipe) + 1 - a) for i in range(n_pipe) for a in range(2)
    ]

    w_block = jnp.pad(w_proj, ((0, PAD - BLOCK), (0, 0)))
    w_own = lax.all_to_all(
        jnp.broadcast_to(w_block[None], (PEERS, PAD, FEATS)), "dp", 0, 0, axis_index_groups=peers, tiled=True
    ).reshape(HALF, FEATS)
    w_other = lax.ppermute(w_own, "dp", swap)

    own_targets = targets[0]
    low = lax.ppermute(own_targets, "dp", upward)
    high = lax.ppermute(own_targets, "dp", downward)
    positions = mask_pos[0, 0] - shard * FRAMES
    next_positions = lax.ppermute(positions, "pipe", back)

    frames = jnp.concatenate([mask_pos[0, 0][None, :], negatives[0, 0]], axis=0) - (shard - 1) * FRAMES
    frames = jnp.pad(frames, ((0, LANES - COLUMNS), (0, 0)), constant_values=-1).T

    rows_own, rows_other, turned_own, turned_other = call(
        rows_body,
        [((SLOTS, HALF), BF16)] * 2 + [((HALF, SLOTS), BF16)] * 2,
        1, 2, flops=3 * 10**9, bytes_accessed=4 * 10**6,
    )(core, positions[:, None], hidden[0])
    turned_got = lax.ppermute(turned_other, "dp", swap)

    column, times = call(
        index_body, [((SLOTS, WINDOW), I32), ((SLOTS, LANES), F32)], 0, 1,
        flops=10**10, bytes_accessed=2 * 10**6,
    )(frames)

    window = jnp.concatenate([low, own_targets, high], axis=0)
    window_f = window.astype(F32)
    norms = jnp.sum(window_f * window_f, axis=1).reshape(TILES, LANES)
    norms = jnp.pad(norms, ((0, 16 - TILES), (0, 0)))

    sent, context = call(
        score_body, [((SLOTS + 16, LANES), F32), ((SLOTS, FEATS), F32)], 0, 7,
        scratch=[pltpu.VMEM((SLOTS, WINDOW), F32)], flops=10**9, bytes_accessed=6 * 10**6,
    )(rows_own, rows_other, w_own, w_other, window, frames, norms)
    got = lax.ppermute(sent, "param", [(0, 1), (1, 0)])

    dctx, unit, step, along = call(
        slots_body,
        [((SLOTS, FEATS), BF16)] * 2 + [((SLOTS, LANES), F32)] * 2,
        1, 7,
        scratch=[pltpu.VMEM((SLOTS, LANES), F32)] * 2 + [pltpu.VMEM((SLOTS, WINDOW), BF16)],
        flops=5 * 10**8, bytes_accessed=5 * 10**6,
    )(mask_counts[0], sent, got, context, frames, times, column, window)
    dctx_got = lax.ppermute(dctx, "dp", swap)

    share = (dot(turned_own, dctx) + dot(turned_got, dctx_got)).astype(BF16)
    shares = lax.all_to_all(
        share.reshape(PEERS, PAD, FEATS), "dp", 0, 0, axis_index_groups=peers, tiled=True
    )
    grad_w = jnp.sum(shares.astype(F32), axis=0)
    grad_w = grad_w + lax.ppermute(grad_w, "pipe", [(i, i ^ 1) for i in range(n_pipe)])
    grad_w = grad_w + lax.ppermute(grad_w, "pipe", [(i, i ^ 2) for i in range(n_pipe)])

    same, cross = call(
        drows_body, [((SLOTS, HALF), BF16)] * 2, 1, 3, flops=10**9, bytes_accessed=3 * 10**6
    )(half, dctx, w_own, w_other)
    same = lax.ppermute(same, "pipe", back)
    cross = lax.ppermute(cross, ("pipe", "param"), back_across)
    (upstream,) = call(
        spread_body, [((FRAMES, MODEL // 2), BF16)], 1, 3, flops=10**9, bytes_accessed=2 * 10**6
    )(core, next_positions[None, :], same, cross)

    to_low, dtgt, to_high, line = call(
        frames_body,
        [((FRAMES + 16, FEATS), BF16), ((FRAMES, FEATS), F32), ((FRAMES + 16, FEATS), BF16), ((8, FRAMES), F32)],
        0, 4,
        scratch=[pltpu.VMEM((SLOTS, WINDOW), BF16), pltpu.VMEM((16, WINDOW), F32)],
        flops=5 * 10**8, bytes_accessed=5 * 10**6,
    )(step, along, column, unit)
    from_low = lax.ppermute(to_high, "dp", upward).astype(F32)
    from_high = lax.ppermute(to_low, "dp", downward).astype(F32)
    dtgt = dtgt + from_low[:FRAMES] + from_high[:FRAMES]
    line = line[0] + jnp.sum(from_low[FRAMES:], axis=0) + jnp.sum(from_high[FRAMES:], axis=0)
    inv_tgt = 1.0 / jnp.sqrt((sent + got)[SLOTS + 4 : SLOTS + 8].reshape(FRAMES) + epsilon)
    grad_t = dtgt * inv_tgt[:, None] - own_targets.astype(F32) * (line * inv_tgt**3)[:, None]
    return (grad_w[:BLOCK], upstream[None], grad_t.astype(BF16)[None])


def solution(mesh):
    return jax.shard_map(
        local,
        mesh=mesh,
        in_specs=(
            P("pipe", "dp", None),
            P("pipe", "dp", "param"),
            P("dp", "param"),
            P("pipe", "dp"),
            P("pipe", "dp", None),
            P("pipe", "dp", None, None),
        ),
        out_specs=(P("dp", "param"), P("pipe", "dp", "param"), P("pipe", "dp", "param")),
        check_vma=False,
    )
```

```python
import jax
import jax.numpy as jnp
from jax import lax
from jax.experimental import pallas as pl
from jax.experimental.pallas import tpu as pltpu
from jax.sharding import PartitionSpec as P

sharpness_divisor = 0.1
loss_multiplier = 32.0
epsilon = 1e-06

F32 = jnp.float32
BF16 = jnp.bfloat16
I32 = jnp.int32

LANES = 128
SLOTS = 256
FRAMES = 512
WINDOW = 3 * FRAMES
TILES = WINDOW // LANES
WORDS = TILES // 4
COLUMNS = 101
SPARE = LANES - 1
GROUP = 64
MODEL = 1920
FEATS = 512
BLOCK = 30
PAD = 32
PEERS = 32
HALF = PEERS * PAD


def iota(shape, dim):
    return lax.broadcasted_iota(I32, shape, dim)


def one_hot(hits):
    return jnp.where(hits, 1.0, 0.0).astype(BF16)


def dot(left, right):
    return jnp.dot(left, right, preferred_element_type=F32)


def dot_cols(left, right):
    return lax.dot_general(left, right, (((1,), (1,)), ((), ())), preferred_element_type=F32)


def dot_rows(left, right):
    return lax.dot_general(left, right, (((0,), (0,)), ((), ())), preferred_element_type=F32)


def lookup(table, index):
    return jnp.take_along_axis(table, index, axis=1, mode="promise_in_bounds")


def call(body, outs, n_scalars, n_arrays, scratch=(), flops=0, bytes_accessed=0, vmem=8):
    return pl.pallas_call(
        body,
        out_shape=tuple(jax.ShapeDtypeStruct(shape, dtype) for shape, dtype in outs),
        in_specs=[pl.BlockSpec(memory_space=pltpu.SMEM)] * n_scalars
        + [pl.BlockSpec(memory_space=pltpu.VMEM)] * n_arrays,
        out_specs=tuple(pl.BlockSpec(memory_space=pltpu.VMEM) for _ in outs),
        scratch_shapes=list(scratch),
        compiler_params=pltpu.CompilerParams(vmem_limit_bytes=vmem * 1024 * 1024),
        cost_estimate=pl.CostEstimate(
            flops=flops, bytes_accessed=bytes_accessed, transcendentals=0
        ),
    )


def blocks_body(w_ref, out_ref):
    block = w_ref[...].astype(F32)
    block = jnp.concatenate([block, jnp.zeros((PAD - BLOCK, FEATS), F32)], axis=0).astype(BF16)
    for i in range(PEERS):
        out_ref[i] = block


def window_body(low_ref, own_ref, high_ref, window_ref, norm_ref):
    norm_ref[...] = jnp.zeros((16, LANES), F32)
    for part, ref in enumerate((low_ref, own_ref, high_ref)):
        for k in range(FRAMES // LANES):
            frames = ref[LANES * k : LANES * (k + 1), :]
            at = part * FRAMES + LANES * k
            window_ref[at : at + LANES, :] = frames
            square = frames.astype(F32)
            square = square * square
            partial = sum(square[:, LANES * i : LANES * (i + 1)] for i in range(FEATS // LANES))
            t = at // LANES
            norm_ref[t : t + 1, :] = jnp.sum(partial.T, axis=0, keepdims=True)


def spans_of(core):
    step = 256
    for side, parity in enumerate((core, 1 - core)):
        for k in range(HALF // step):
            low = (2 * BLOCK * step // PAD * k) // LANES * LANES
            wide = min(MODEL, low + 640) - low
            q = iota((step, wide), 0) + step * k
            wanted = BLOCK * (2 * (q >> 5) + parity) + (q & 31)
            spread = one_hot((wanted == iota((step, wide), 1) + low) & ((q & 31) < BLOCK))
            yield side, slice(step * k, step * (k + 1)), slice(low, low + wide), spread


def rows_body(core_ref, pos_ref, hidden_ref, own_ref, other_ref, rows_ref):
    chosen = one_hot(pos_ref[...] == iota((SLOTS, FRAMES), 1))
    rows = dot(chosen, hidden_ref[...]).astype(BF16)
    rows_ref[...] = rows
    for side, to, of, spread in spans_of(core_ref[0]):
        (own_ref, other_ref)[side][:, to] = dot_cols(rows[:, of], spread).astype(BF16)


def turned_body(core_ref, rows_ref, own_ref, other_ref):
    for side, to, of, spread in spans_of(core_ref[0]):
        (own_ref, other_ref)[side][to, :] = dot_cols(spread, rows_ref[:, of]).astype(BF16)


def index_body(named_ref, packed_ref, times_ref, frame_ref, words_ref):
    depth = 32
    here_at, times_at = WORDS, WORDS + 1
    for side in range(SLOTS // LANES):
        across = slice(LANES * side, LANES * (side + 1))

        def prepare(i, carry):
            rows = pl.ds(pl.multiple_of(i * depth, depth), depth)
            part = named_ref[rows, across]
            times = jnp.zeros((depth, LANES), I32)
            first = jnp.full((depth, LANES), SPARE, I32)
            for c in reversed(range(COLUMNS)):
                same = part == jnp.broadcast_to(named_ref[c : c + 1, across], (depth, LANES))
                times = times + jnp.where(same, 1, 0)
                first = jnp.where(same, c, first)
            mine = iota((depth, LANES), 0) + i * depth
            tile = part >> 7
            value = jnp.where((first == mine) & (mine < COLUMNS), (SPARE - mine) << ((tile & 3) * 8), 0)
            for w in range(WORDS):
                words_ref[w, rows, across] = jnp.where((tile >> 2) == w, value, 0)
            words_ref[here_at, rows, across] = part & 127
            words_ref[times_at, rows, across] = times
            return carry

        def pack(i, carry):
            rows = pl.ds(pl.multiple_of(i * depth, depth), depth)
            place = iota((depth, LANES), 0) + i * depth
            packed = [jnp.zeros((depth, LANES), I32) for _ in range(WORDS)]
            for c in range(COLUMNS):
                here = place == jnp.broadcast_to(words_ref[here_at, c : c + 1, across], (depth, LANES))
                for w in range(WORDS):
                    word = jnp.broadcast_to(words_ref[w, c : c + 1, across], (depth, LANES))
                    packed[w] = packed[w] + jnp.where(here, word, 0)
            for w in range(WORDS):
                words_ref[times_at + 1 + w, rows, across] = packed[w]
            return carry

        lax.fori_loop(0, LANES // depth, prepare, 0)
        lax.fori_loop(0, LANES // depth, pack, 0)
        times_ref[across, :] = words_ref[times_at, :, across].T.astype(F32)
        frame_ref[across, :] = named_ref[:, across].T
        for w in range(WORDS):
            packed_ref[across, LANES * w : LANES * (w + 1)] = words_ref[times_at + 1 + w, :, across].T


def columns_of(packed_ref, rows):
    for w in range(WORDS):
        word = packed_ref[rows, LANES * w : LANES * (w + 1)]
        for k in range(4):
            yield 4 * w + k, SPARE - ((word >> (8 * k)) & 127)


def part_body(rows_ref, w_ref, out_ref):
    out_ref[...] = dot(rows_ref[...], w_ref[...])


def score_body(part_ref, other_ref, w_other_ref, window_ref, frame_ref, norm_ref, sent_ref, context_ref, table_ref):
    context = part_ref[...] + dot(other_ref[...], w_other_ref[...])
    context_ref[...] = context
    table_ref[...] = dot_cols(context.astype(BF16), window_ref[...])
    sent_ref[0:SLOTS, :] = jnp.broadcast_to(
        jnp.sum(context * context, axis=1, keepdims=True), (SLOTS, LANES)
    )
    sent_ref[SLOTS : SLOTS + 16, :] = norm_ref[...]
    lane = iota((GROUP, LANES), 1)

    def group(g, carry):
        rows = pl.ds(pl.multiple_of(g * GROUP, GROUP), GROUP)
        frame = frame_ref[rows, :]
        tile, place = frame >> 7, frame & 127
        picked = jnp.where(lane == COLUMNS, sent_ref[rows, :], 0.0)
        for t in range(TILES):
            found = lookup(table_ref[rows, LANES * t : LANES * (t + 1)], place)
            picked = jnp.where((tile == t) & (lane < COLUMNS), found, picked)
        sent_ref[rows, :] = picked
        return carry

    lax.fori_loop(0, SLOTS // GROUP, group, 0)


def slots_body(
    count_ref, place_ref, sent_ref, got_ref, context_ref, frame_ref, times_ref, packed_ref, window_ref,
    dctx_ref, unit_ref, step_ref, along_ref, inverse_ref, shift_ref, scores_ref,
):
    inv_tgt = 1.0 / jnp.sqrt(
        sent_ref[SLOTS : SLOTS + 16, :] + got_ref[SLOTS : SLOTS + 16, :] + epsilon
    )
    lane = iota((GROUP, LANES), 1)
    named = lane < COLUMNS
    count = count_ref[0]

    def group(g, carry):
        rows = pl.ds(pl.multiple_of(g * GROUP, GROUP), GROUP)
        raw = sent_ref[rows, :] + got_ref[rows, :]
        inverse = 1.0 / jnp.sqrt(raw[:, COLUMNS : COLUMNS + 1] + epsilon)
        frame = frame_ref[rows, :]
        tile, place = frame >> 7, frame & 127
        scale = jnp.zeros((GROUP, LANES), F32)
        for t in range(TILES):
            line = jnp.broadcast_to(inv_tgt[t : t + 1, :], (GROUP, LANES))
            scale = jnp.where(tile == t, lookup(line, place), scale)
        logits = raw * inverse * scale / sharpness_divisor
        expon = jnp.where(named, jnp.exp(jnp.where(named, logits, 0.0)), 0.0)
        probs = expon / jnp.sum(expon, axis=1, keepdims=True)
        live = iota((GROUP, LANES), 0) + g * GROUP < count
        first = jnp.where(lane == 0, 1.0, 0.0)
        step = jnp.where(live & named, loss_multiplier * (probs - first) / sharpness_divisor, 0.0)
        times = jnp.maximum(times_ref[rows, :], 1.0)
        step = step * times
        weight = (step * scale).astype(BF16).astype(F32)
        along = jnp.sum(jnp.where(named, weight * raw / times, 0.0), axis=1, keepdims=True)
        step_ref[rows, :] = step
        along_ref[rows, :] = jnp.where(named, step.astype(BF16).astype(F32) * raw * inverse, 0.0)
        inverse_ref[rows, :] = jnp.broadcast_to(inverse, (GROUP, LANES))
        shift_ref[rows, :] = jnp.broadcast_to(along * inverse * inverse * inverse, (GROUP, LANES))
        for t, column in columns_of(packed_ref, rows):
            scores_ref[rows, LANES * t : LANES * (t + 1)] = lookup(weight, column).astype(BF16)
        return carry

    lax.fori_loop(0, SLOTS // GROUP, group, 0)
    context = context_ref[...]
    inverse = inverse_ref[:, 0:1]
    dunit = dot(scores_ref[...], window_ref[...])
    dctx_ref[0:SLOTS, :] = (dunit * inverse - context * shift_ref[:, 0:1]).astype(BF16)
    places = jnp.broadcast_to(place_ref[...], (16, SLOTS))
    parts = jnp.where(iota((16, SLOTS), 0) == 0, places >> 4, places & 15)
    dctx_ref[SLOTS : SLOTS + 16, :] = jnp.zeros((16, FEATS), BF16)
    dctx_ref[SLOTS : SLOTS + 16, 0:SLOTS] = parts.astype(F32).astype(BF16)
    unit_ref[...] = (context * inverse).astype(BF16)


def frames_body(step_ref, along_ref, packed_ref, unit_ref, low_ref, own_ref, high_ref, line_ref, scores_ref, sums_ref):
    sums_ref[...] = jnp.zeros((8, WINDOW), F32)

    def group(g, carry):
        rows = pl.ds(pl.multiple_of(g * GROUP, GROUP), GROUP)
        step = step_ref[rows, :]
        along = along_ref[rows, :]
        for t, column in columns_of(packed_ref, rows):
            span = slice(LANES * t, LANES * (t + 1))
            scores_ref[rows, span] = lookup(step, column).astype(BF16)
            sums_ref[:, span] += jnp.sum(lookup(along, column).reshape(GROUP // 8, 8, LANES), axis=0)
        return carry

    lax.fori_loop(0, SLOTS // GROUP, group, 0)
    line = jnp.sum(sums_ref[...], axis=0, keepdims=True)
    line_ref[...] = jnp.broadcast_to(line[:, FRAMES : 2 * FRAMES], (8, FRAMES))
    row = iota((16, FRAMES), 0)
    for part, ref in ((0, low_ref), (1, own_ref), (2, high_ref)):
        span = slice(FRAMES * part, FRAMES * (part + 1))
        ref[0:FRAMES, :] = dot_rows(scores_ref[:, span], unit_ref[...]).astype(ref.dtype)
        if part != 1:
            left = jnp.broadcast_to(line[:, span], (16, FRAMES))
            first = left.astype(BF16).astype(F32)
            second = (left - first).astype(BF16).astype(F32)
            third = left - first - second
            ref[FRAMES : FRAMES + 16, :] = jnp.where(
                row == 0, first, jnp.where(row == 1, second, jnp.where(row == 2, third, 0.0))
            ).astype(BF16)


def share_body(turned_own_ref, turned_got_ref, own_ref, got_ref, out_ref):
    own = dot(turned_own_ref[...], own_ref[0:SLOTS, :])
    out_ref[...] = (own + dot(turned_got_ref[...], got_ref[0:SLOTS, :])).astype(BF16)


def total_body(parts_ref, out_ref):
    total = jnp.sum(parts_ref[...].astype(F32), axis=0)
    for i in range(out_ref.shape[0]):
        out_ref[i] = total


def sum_body(parts_ref, out_ref):
    out_ref[...] = jnp.sum(parts_ref[...], axis=0)[0:BLOCK, :]


def cross_body(half_ref, dctx_ref, w_own_ref, w_other_ref, cross_ref):
    rows = pl.ds(pl.multiple_of((1 - half_ref[0]) * (HALF // 2), HALF // 2), HALF // 2)
    dctx = dctx_ref[0:SLOTS, :]
    cross_ref[:, 0 : HALF // 2] = dot_cols(dctx, w_own_ref[rows, :]).astype(BF16)
    cross_ref[:, HALF // 2 : HALF] = dot_cols(dctx, w_other_ref[rows, :]).astype(BF16)


def spread_body(core_ref, half_ref, same_ref, cross_ref, w_own_ref, w_other_ref, line_ref, out_ref, rows_ref):
    core = core_ref[0]
    which = pl.ds(pl.multiple_of(half_ref[0] * (HALF // 2), HALF // 2), HALF // 2)
    dctx = same_ref[0:SLOTS, :]
    parts = same_ref[SLOTS : SLOTS + 16, 0:SLOTS].astype(F32)
    places = (parts[0:1, :] * 16.0 + parts[1:2, :]).astype(I32)
    placed = one_hot(iota((FRAMES, SLOTS), 0) == places)
    rows_ref[...] = jnp.zeros((SLOTS, MODEL // 2), F32)
    step = 256
    for side, (parity, w_ref) in enumerate(((core, w_own_ref), (1 - core, w_other_ref))):
        span = slice(HALF // 2 * side, HALF // 2 * (side + 1))
        drows = (dot_cols(dctx, w_ref[which, :]) + cross_ref[:, span].astype(F32)).astype(BF16)
        for k in range(HALF // 2 // step):
            first = 2 * BLOCK * step // PAD * k
            low = first // LANES * LANES
            high = min(MODEL // 2, -(-(first + 2 * BLOCK * step // PAD) // LANES) * LANES)
            q = iota((step, high - low), 0) + step * k
            wanted = BLOCK * (2 * (q >> 5) + parity) + (q & 31)
            unpad = one_hot((wanted == iota((step, high - low), 1) + low) & ((q & 31) < BLOCK))
            rows_ref[:, low:high] += dot(drows[:, step * k : step * (k + 1)], unpad)
    out_ref[...] = dot(placed, rows_ref[...].astype(BF16)).astype(BF16)


def targets_body(targets_ref, own_ref, low_ref, high_ref, line_ref, sent_ref, got_ref, out_ref):
    tail = slice(FRAMES, FRAMES + 16)
    line = line_ref[0:1, :] + jnp.sum(
        low_ref[tail, :].astype(F32) + high_ref[tail, :].astype(F32), axis=0, keepdims=True
    )
    inv_tgt = 1.0 / jnp.sqrt(
        sent_ref[SLOTS : SLOTS + 16, :] + got_ref[SLOTS : SLOTS + 16, :] + epsilon
    )
    for t in range(FRAMES // LANES):
        span = slice(LANES * t, LANES * (t + 1))
        scale = inv_tgt[TILES // 3 + t : TILES // 3 + t + 1, :]
        shift = line[:, span] * scale * scale * scale
        scale = jnp.broadcast_to(scale, (LANES, LANES)).T[:, 0:1]
        shift = jnp.broadcast_to(shift, (LANES, LANES)).T[:, 0:1]
        dtgt = own_ref[span, :] + low_ref[span, :].astype(F32) + high_ref[span, :].astype(F32)
        out_ref[span, :] = (dtgt * scale - targets_ref[span, :].astype(F32) * shift).astype(BF16)


def local(hidden, targets, w_proj, mask_counts, mask_pos, negatives):
    shard = lax.axis_index("dp")
    core = (shard % 2).astype(I32).reshape(1)
    half = lax.axis_index("param").astype(I32).reshape(1)
    n_dp = lax.axis_size("dp")
    n_pipe = lax.axis_size("pipe")
    peers = [[2 * i + c for i in range(n_dp // 2)] for c in range(2)]
    swap = [(i, i ^ 1) for i in range(n_dp)]
    upward = [(i, i + 1) for i in range(n_dp - 1)]
    downward = [(i + 1, i) for i in range(n_dp - 1)]
    back = [(i, (i - 1) % n_pipe) for i in range(n_pipe)]
    back_across = [
        (2 * i + a, 2 * ((i - 1) % n_pipe) + 1 - a) for i in range(n_pipe) for a in range(2)
    ]

    (w_blocks,) = call(blocks_body, [((PEERS, PAD, FEATS), BF16)], 0, 1, bytes_accessed=10**6)(w_proj)
    w_own = lax.all_to_all(w_blocks, "dp", 0, 0, axis_index_groups=peers, tiled=True).reshape(HALF, FEATS)
    own_targets = targets[0]
    low = lax.ppermute(own_targets, "dp", upward)
    high = lax.ppermute(own_targets, "dp", downward)
    positions = mask_pos[0, 0] - shard * FRAMES

    frames = jnp.concatenate([mask_pos[0, 0][None, :], negatives[0, 0]], axis=0) - (shard - 1) * FRAMES
    frames = jnp.pad(frames, ((0, LANES - COLUMNS), (0, 0)), constant_values=-1)

    rows_own, rows_other, rows = call(
        rows_body,
        [((SLOTS, HALF), BF16)] * 2 + [((SLOTS, MODEL), BF16)],
        1, 2, flops=2 * 10**9, bytes_accessed=4 * 10**6,
    )(core, positions[:, None], hidden[0])
    turned_own, turned_other = call(
        turned_body, [((HALF, SLOTS), BF16)] * 2, 1, 1, flops=10**9, bytes_accessed=2 * 10**6
    )(core, rows)
    turned_got = lax.ppermute(turned_other, "dp", swap)

    packed, times, frames = call(
        index_body, [((SLOTS, WORDS * LANES), I32), ((SLOTS, LANES), F32), ((SLOTS, LANES), I32)], 0, 1,
        scratch=[pltpu.VMEM((2 * WORDS + 2, LANES, SLOTS), I32)], flops=5 * 10**9, bytes_accessed=10**6,
    )(frames)

    window, norms = call(
        window_body, [((WINDOW, FEATS), BF16), ((16, LANES), F32)], 0, 3, flops=10**6, bytes_accessed=3 * 10**6
    )(low, own_targets, high)
    w_own, rows_own, rows_other, turned_own, turned_got, packed, times, frames, window, norms = lax.optimization_barrier(
        (w_own, rows_own, rows_other, turned_own, turned_got, packed, times, frames, window, norms)
    )
    w_other = lax.ppermute(w_own, "dp", swap)

    (part,) = call(
        part_body, [((SLOTS, FEATS), F32)], 0, 2, flops=3 * 10**8, bytes_accessed=2 * 10**6
    )(rows_own, w_own)
    sent, context = call(
        score_body, [((SLOTS + 16, LANES), F32), ((SLOTS, FEATS), F32)], 0, 6,
        scratch=[pltpu.VMEM((SLOTS, WINDOW), F32)], flops=10**9, bytes_accessed=6 * 10**6,
    )(part, rows_other, w_other, window, frames, norms)
    got = lax.ppermute(sent, "param", [(0, 1), (1, 0)])

    dctx, unit, step, along = call(
        slots_body,
        [((SLOTS + 16, FEATS), BF16), ((SLOTS, FEATS), BF16)] + [((SLOTS, LANES), F32)] * 2,
        1, 8,
        scratch=[pltpu.VMEM((SLOTS, LANES), F32)] * 2 + [pltpu.VMEM((SLOTS, WINDOW), BF16)],
        flops=5 * 10**8, bytes_accessed=5 * 10**6,
    )(mask_counts[0], positions[None, :], sent, got, context, frames, times, packed, window)
    dctx_got = lax.ppermute(dctx, "dp", swap)

    (share,) = call(
        share_body, [((HALF, FEATS), BF16)], 0, 4, flops=5 * 10**8, bytes_accessed=3 * 10**6
    )(turned_own, turned_got, dctx, dctx_got)
    shares = lax.all_to_all(
        share.reshape(PEERS, PAD, FEATS), "dp", 0, 0, axis_index_groups=peers, tiled=True
    )
    same = lax.ppermute(dctx, "pipe", back)
    shares, same = lax.optimization_barrier((shares, same))
    (copies,) = call(
        total_body, [((n_pipe, PAD, FEATS), F32)], 0, 1, flops=10**6, bytes_accessed=10**6
    )(shares)

    to_low, dtgt, to_high, line = call(
        frames_body,
        [((FRAMES + 16, FEATS), BF16), ((FRAMES, FEATS), F32), ((FRAMES + 16, FEATS), BF16), ((8, FRAMES), F32)],
        0, 4,
        scratch=[pltpu.VMEM((SLOTS, WINDOW), BF16), pltpu.VMEM((8, WINDOW), F32)],
        flops=5 * 10**8, bytes_accessed=5 * 10**6,
    )(step, along, packed, unit)
    from_low = lax.ppermute(to_high, "dp", upward)
    from_high = lax.ppermute(to_low, "dp", downward)

    (cross,) = call(
        cross_body, [((SLOTS, HALF), BF16)], 1, 3, flops=5 * 10**8, bytes_accessed=2 * 10**6
    )(half, dctx, w_own, w_other)
    cross = lax.ppermute(cross, ("pipe", "param"), back_across)

    pipe_parts = lax.all_to_all(copies, "pipe", 0, 0, tiled=True)
    _, line = lax.optimization_barrier((copies, line))
    (grad_t,) = call(
        targets_body, [((FRAMES, FEATS), BF16)], 0, 7, flops=10**7, bytes_accessed=3 * 10**6
    )(own_targets, dtgt, from_low, from_high, line, sent, got)
    cross, _ = lax.optimization_barrier((cross, grad_t))
    (upstream,) = call(
        spread_body, [((FRAMES, MODEL // 2), BF16)], 2, 5,
        scratch=[pltpu.VMEM((SLOTS, MODEL // 2), F32)], flops=10**9, bytes_accessed=4 * 10**6,
    )(core, half, same, cross, w_own, w_other, line)
    (grad_w,) = call(sum_body, [((BLOCK, FEATS), F32)], 0, 1, flops=10**5, bytes_accessed=10**5)(pipe_parts)
    return (grad_w, upstream[None], grad_t[None])


def solution(mesh):
    return jax.shard_map(
        local,
        mesh=mesh,
        in_specs=(
            P("pipe", "dp", None),
            P("pipe", "dp", "param"),
            P("dp", "param"),
            P("pipe", "dp"),
            P("pipe", "dp", None),
            P("pipe", "dp", None, None),
        ),
        out_specs=(P("dp", "param"), P("pipe", "dp", "param"), P("pipe", "dp", "param")),
        check_vma=False,
    )
```

```python
import jax
import jax.numpy as jnp
from jax import lax
from jax.experimental import pallas as pl
from jax.experimental.pallas import tpu as pltpu
from jax.sharding import PartitionSpec as P

sharpness_divisor = 0.1
loss_multiplier = 32.0
epsilon = 1e-06

F32 = jnp.float32
BF16 = jnp.bfloat16
I32 = jnp.int32

LANES = 128
SLOTS = 256
FRAMES = 512
WINDOW = 3 * FRAMES
TILES = WINDOW // LANES
WORDS = TILES // 4
COLUMNS = 101
SPARE = LANES - 1
GROUP = 64
MODEL = 1920
FEATS = 512
BLOCK = 30
PAD = 32
PEERS = 32
HALF = PEERS * PAD
X_CHIPS = 4
Z_CHIPS = 8
QUARTER = HALF // X_CHIPS // 2


def iota(shape, dim):
    return lax.broadcasted_iota(I32, shape, dim)


def one_hot(hits):
    return jnp.where(hits, 1.0, 0.0).astype(BF16)


def dot(left, right):
    return jnp.dot(left, right, preferred_element_type=F32)


def dot_cols(left, right):
    return lax.dot_general(left, right, (((1,), (1,)), ((), ())), preferred_element_type=F32)


def dot_rows(left, right):
    return lax.dot_general(left, right, (((0,), (0,)), ((), ())), preferred_element_type=F32)


def lookup(table, index):
    return jnp.take_along_axis(table, index, axis=1, mode="promise_in_bounds")


def call(body, outs, n_scalars, n_arrays, scratch=(), flops=0, bytes_accessed=0, vmem=8, n_far=0):
    return pl.pallas_call(
        body,
        out_shape=tuple(jax.ShapeDtypeStruct(shape, dtype) for shape, dtype in outs),
        in_specs=[pl.BlockSpec(memory_space=pltpu.SMEM)] * n_scalars
        + [pl.BlockSpec(memory_space=pltpu.VMEM)] * n_arrays
        + [pl.BlockSpec(memory_space=pl.ANY)] * n_far,
        out_specs=tuple(pl.BlockSpec(memory_space=pltpu.VMEM) for _ in outs),
        scratch_shapes=list(scratch),
        compiler_params=pltpu.CompilerParams(vmem_limit_bytes=vmem * 1024 * 1024),
        cost_estimate=pl.CostEstimate(
            flops=flops, bytes_accessed=bytes_accessed, transcendentals=0
        ),
    )


def blocks_body(w_ref, out_ref):
    block = w_ref[...].astype(F32)
    block = jnp.concatenate([block, jnp.zeros((PAD - BLOCK, FEATS), F32)], axis=0).astype(BF16)
    for i in range(PEERS):
        out_ref[i] = block


def window_body(low_ref, own_ref, high_ref, window_ref, norm_ref):
    norm_ref[...] = jnp.zeros((16, LANES), F32)
    for part, ref in enumerate((low_ref, own_ref, high_ref)):
        for k in range(FRAMES // LANES):
            frames = ref[LANES * k : LANES * (k + 1), :]
            at = part * FRAMES + LANES * k
            window_ref[at : at + LANES, :] = frames
            square = frames.astype(F32)
            square = square * square
            partial = sum(square[:, LANES * i : LANES * (i + 1)] for i in range(FEATS // LANES))
            t = at // LANES
            norm_ref[t : t + 1, :] = jnp.sum(partial.T, axis=0, keepdims=True)


def rows_body(core_ref, pos_ref, hidden_ref, own_ref, other_ref, own_t_ref, other_t_ref, turn_ref):
    chosen = one_hot(pos_ref[...] == iota((SLOTS, FRAMES), 1))
    rows = dot(chosen, hidden_ref[...]).astype(BF16)
    core = core_ref[0]
    step = 256
    for parity, straight, turned in ((core, own_ref, own_t_ref), (1 - core, other_ref, other_t_ref)):
        for k in range(HALF // step):
            low = (2 * BLOCK * step // PAD * k) // LANES * LANES
            wide = min(MODEL, low + 640) - low
            q = iota((step, wide), 0) + step * k
            wanted = BLOCK * (2 * (q >> 5) + parity) + (q & 31)
            spread = one_hot((wanted == iota((step, wide), 1) + low) & ((q & 31) < BLOCK))
            piece = dot_cols(spread, rows[:, low : low + wide])
            for i in range(step // PAD):
                z, x = divmod(step // PAD * k + i, X_CHIPS)
                at = PAD * (x * Z_CHIPS + z)
                turn_ref[at : at + PAD, :] = piece[PAD * i : PAD * (i + 1), :]
        turned[...] = turn_ref[...].astype(BF16)
        for g in range(HALF // LANES):
            span = slice(LANES * g, LANES * (g + 1))
            straight[:, span] = turn_ref[span, :].T.astype(BF16)


def index_body(named_ref, packed_ref, times_ref, frame_ref, words_ref):
    depth = 32
    here_at, times_at = WORDS, WORDS + 1
    for side in range(SLOTS // LANES):
        across = slice(LANES * side, LANES * (side + 1))

        def prepare(i, carry):
            rows = pl.ds(pl.multiple_of(i * depth, depth), depth)
            part = named_ref[rows, across]
            times = jnp.zeros((depth, LANES), I32)
            first = jnp.full((depth, LANES), SPARE, I32)
            for c in reversed(range(COLUMNS)):
                same = part == jnp.broadcast_to(named_ref[c : c + 1, across], (depth, LANES))
                times = times + jnp.where(same, 1, 0)
                first = jnp.where(same, c, first)
            mine = iota((depth, LANES), 0) + i * depth
            tile = part >> 7
            value = jnp.where((first == mine) & (mine < COLUMNS), (SPARE - mine) << ((tile & 3) * 8), 0)
            for w in range(WORDS):
                words_ref[w, rows, across] = jnp.where((tile >> 2) == w, value, 0)
            words_ref[here_at, rows, across] = part & 127
            words_ref[times_at, rows, across] = times
            return carry

        def pack(i, carry):
            rows = pl.ds(pl.multiple_of(i * depth, depth), depth)
            place = iota((depth, LANES), 0) + i * depth
            packed = [jnp.zeros((depth, LANES), I32) for _ in range(WORDS)]
            for c in range(COLUMNS):
                here = place == jnp.broadcast_to(words_ref[here_at, c : c + 1, across], (depth, LANES))
                for w in range(WORDS):
                    word = jnp.broadcast_to(words_ref[w, c : c + 1, across], (depth, LANES))
                    packed[w] = packed[w] + jnp.where(here, word, 0)
            for w in range(WORDS):
                words_ref[times_at + 1 + w, rows, across] = packed[w]
            return carry

        lax.fori_loop(0, LANES // depth, prepare, 0)
        lax.fori_loop(0, LANES // depth, pack, 0)
        times_ref[across, :] = words_ref[times_at, :, across].T.astype(F32)
        frame_ref[across, :] = named_ref[:, across].T
        for w in range(WORDS):
            packed_ref[across, LANES * w : LANES * (w + 1)] = words_ref[times_at + 1 + w, :, across].T


def columns_of(packed_ref, rows):
    for w in range(WORDS):
        word = packed_ref[rows, LANES * w : LANES * (w + 1)]
        for k in range(4):
            yield 4 * w + k, SPARE - ((word >> (8 * k)) & 127)


def part_body(rows_ref, w_ref, out_ref):
    out_ref[...] = dot(rows_ref[...], w_ref[...])


def score_body(part_ref, other_ref, w_other_ref, window_ref, frame_ref, norm_ref, sent_ref, context_ref, table_ref):
    context = part_ref[...] + dot(other_ref[...], w_other_ref[...])
    context_ref[...] = context
    table_ref[...] = dot_cols(context.astype(BF16), window_ref[...])
    sent_ref[0:SLOTS, :] = jnp.broadcast_to(
        jnp.sum(context * context, axis=1, keepdims=True), (SLOTS, LANES)
    )
    sent_ref[SLOTS : SLOTS + 16, :] = norm_ref[...]
    lane = iota((GROUP, LANES), 1)

    def group(g, carry):
        rows = pl.ds(pl.multiple_of(g * GROUP, GROUP), GROUP)
        frame = frame_ref[rows, :]
        tile, place = frame >> 7, frame & 127
        picked = jnp.where(lane == COLUMNS, sent_ref[rows, :], 0.0)
        for t in range(TILES):
            found = lookup(table_ref[rows, LANES * t : LANES * (t + 1)], place)
            picked = jnp.where((tile == t) & (lane < COLUMNS), found, picked)
        sent_ref[rows, :] = picked
        return carry

    lax.fori_loop(0, SLOTS // GROUP, group, 0)


def slots_body(
    count_ref, place_ref, sent_ref, got_ref, context_ref, frame_ref, times_ref, packed_ref, window_ref,
    dctx_ref, unit_ref, step_ref, along_ref, inverse_ref, shift_ref, scores_ref,
):
    inv_tgt = 1.0 / jnp.sqrt(
        sent_ref[SLOTS : SLOTS + 16, :] + got_ref[SLOTS : SLOTS + 16, :] + epsilon
    )
    lane = iota((GROUP, LANES), 1)
    named = lane < COLUMNS
    count = count_ref[0]

    def group(g, carry):
        rows = pl.ds(pl.multiple_of(g * GROUP, GROUP), GROUP)
        raw = sent_ref[rows, :] + got_ref[rows, :]
        inverse = 1.0 / jnp.sqrt(raw[:, COLUMNS : COLUMNS + 1] + epsilon)
        frame = frame_ref[rows, :]
        tile, place = frame >> 7, frame & 127
        scale = jnp.zeros((GROUP, LANES), F32)
        for t in range(TILES):
            line = jnp.broadcast_to(inv_tgt[t : t + 1, :], (GROUP, LANES))
            scale = jnp.where(tile == t, lookup(line, place), scale)
        logits = raw * inverse * scale / sharpness_divisor
        expon = jnp.where(named, jnp.exp(jnp.where(named, logits, 0.0)), 0.0)
        probs = expon / jnp.sum(expon, axis=1, keepdims=True)
        live = iota((GROUP, LANES), 0) + g * GROUP < count
        first = jnp.where(lane == 0, 1.0, 0.0)
        step = jnp.where(live & named, loss_multiplier * (probs - first) / sharpness_divisor, 0.0)
        times = jnp.maximum(times_ref[rows, :], 1.0)
        step = step * times
        weight = (step * scale).astype(BF16).astype(F32)
        along = jnp.sum(jnp.where(named, weight * raw / times, 0.0), axis=1, keepdims=True)
        step_ref[rows, :] = step
        along_ref[rows, :] = jnp.where(named, step.astype(BF16).astype(F32) * raw * inverse, 0.0)
        inverse_ref[rows, :] = jnp.broadcast_to(inverse, (GROUP, LANES))
        shift_ref[rows, :] = jnp.broadcast_to(along * inverse * inverse * inverse, (GROUP, LANES))
        for t, column in columns_of(packed_ref, rows):
            scores_ref[rows, LANES * t : LANES * (t + 1)] = lookup(weight, column).astype(BF16)
        return carry

    lax.fori_loop(0, SLOTS // GROUP, group, 0)
    context = context_ref[...]
    inverse = inverse_ref[:, 0:1]
    dunit = dot(scores_ref[...], window_ref[...])
    dctx_ref[0:SLOTS, :] = (dunit * inverse - context * shift_ref[:, 0:1]).astype(BF16)
    places = jnp.broadcast_to(place_ref[...], (16, SLOTS))
    parts = jnp.where(iota((16, SLOTS), 0) == 0, places >> 4, places & 15)
    dctx_ref[SLOTS : SLOTS + 16, :] = jnp.zeros((16, FEATS), BF16)
    dctx_ref[SLOTS : SLOTS + 16, 0:SLOTS] = parts.astype(F32).astype(BF16)
    unit_ref[...] = (context * inverse).astype(BF16)


def frames_body(step_ref, along_ref, packed_ref, unit_ref, low_ref, own_ref, high_ref, line_ref, scores_ref, sums_ref):
    sums_ref[...] = jnp.zeros((8, WINDOW), F32)

    def group(g, carry):
        rows = pl.ds(pl.multiple_of(g * GROUP, GROUP), GROUP)
        step = step_ref[rows, :]
        along = along_ref[rows, :]
        for t, column in columns_of(packed_ref, rows):
            span = slice(LANES * t, LANES * (t + 1))
            scores_ref[rows, span] = lookup(step, column).astype(BF16)
            sums_ref[:, span] += jnp.sum(lookup(along, column).reshape(GROUP // 8, 8, LANES), axis=0)
        return carry

    lax.fori_loop(0, SLOTS // GROUP, group, 0)
    line = jnp.sum(sums_ref[...], axis=0, keepdims=True)
    line_ref[...] = jnp.broadcast_to(line[:, FRAMES : 2 * FRAMES], (8, FRAMES))
    row = iota((16, FRAMES), 0)
    for part, ref in ((0, low_ref), (1, own_ref), (2, high_ref)):
        span = slice(FRAMES * part, FRAMES * (part + 1))
        ref[0:FRAMES, :] = dot_rows(scores_ref[:, span], unit_ref[...]).astype(ref.dtype)
        if part != 1:
            left = jnp.broadcast_to(line[:, span], (16, FRAMES))
            first = left.astype(BF16).astype(F32)
            second = (left - first).astype(BF16).astype(F32)
            third = left - first - second
            ref[FRAMES : FRAMES + 16, :] = jnp.where(
                row == 0, first, jnp.where(row == 1, second, jnp.where(row == 2, third, 0.0))
            ).astype(BF16)


def share_body(turned_own_ref, turned_got_ref, own_ref, got_ref, out_ref):
    own = dot(turned_own_ref[...], own_ref[0:SLOTS, :])
    out_ref[...] = (own + dot(turned_got_ref[...], got_ref[0:SLOTS, :])).astype(BF16)


def merge_body(parts_ref, out_ref):
    out_ref[...] = jnp.sum(parts_ref[...].astype(F32), axis=0).astype(BF16)


def token_body(cross_ref, same_ref, out_ref):
    out_ref[...] = jnp.zeros((8, LANES), F32)


def total_body(parts_ref, token_ref, out_ref):
    total = jnp.sum(parts_ref[...].astype(F32), axis=0)
    for i in range(out_ref.shape[0]):
        out_ref[i] = total


def sum_body(parts_ref, out_ref):
    out_ref[...] = jnp.sum(parts_ref[...], axis=0)[0:BLOCK, :]


def half_of(w_ref, half):
    return jnp.concatenate(
        [
            w_ref[pl.ds(pl.multiple_of(2 * QUARTER * x + half * QUARTER, QUARTER), QUARTER), :]
            for x in range(X_CHIPS)
        ],
        axis=0,
    )


def cross_body(half_ref, dctx_ref, w_own_ref, w_other_ref, cross_ref):
    half = 1 - half_ref[0]
    dctx = dctx_ref[0:SLOTS, :]
    cross_ref[:, 0 : HALF // 2] = dot_cols(dctx, half_of(w_own_ref, half)).astype(BF16)
    cross_ref[:, HALF // 2 : HALF] = dot_cols(dctx, half_of(w_other_ref, half)).astype(BF16)


def spread_body(core_ref, half_ref, same_ref, cross_ref, w_own_ref, w_other_ref, line_ref, out_ref):
    core = core_ref[0]
    dctx = same_ref[0:SLOTS, :]
    parts = same_ref[SLOTS : SLOTS + 16, 0:SLOTS].astype(F32)
    places = (parts[0:1, :] * 16.0 + parts[1:2, :]).astype(I32)
    placed = one_hot(iota((FRAMES, SLOTS), 0) == places)
    shape = (HALF // 2, MODEL // 2)
    rows = jnp.zeros((SLOTS, MODEL // 2), F32)
    for side, (parity, w_ref) in enumerate(((core, w_own_ref), (1 - core, w_other_ref))):
        span = slice(HALF // 2 * side, HALF // 2 * (side + 1))
        drows = (dot_cols(dctx, half_of(w_ref, half_ref[0])) + cross_ref[:, span].astype(F32)).astype(BF16)
        q = iota(shape, 0)
        block = 2 * (X_CHIPS * ((q >> 5) & (Z_CHIPS // 2 - 1)) + (q >> 7)) + parity
        unpad = one_hot((BLOCK * block + (q & 31) == iota(shape, 1)) & ((q & 31) < BLOCK))
        rows = rows + dot(drows, unpad)
    out_ref[...] = dot(placed, rows.astype(BF16)).astype(BF16)


def targets_body(targets_ref, own_ref, low_ref, high_ref, line_ref, sent_ref, got_ref, out_ref):
    tail = slice(FRAMES, FRAMES + 16)
    line = line_ref[0:1, :] + jnp.sum(
        low_ref[tail, :].astype(F32) + high_ref[tail, :].astype(F32), axis=0, keepdims=True
    )
    inv_tgt = 1.0 / jnp.sqrt(
        sent_ref[SLOTS : SLOTS + 16, :] + got_ref[SLOTS : SLOTS + 16, :] + epsilon
    )
    for t in range(FRAMES // LANES):
        span = slice(LANES * t, LANES * (t + 1))
        scale = inv_tgt[TILES // 3 + t : TILES // 3 + t + 1, :]
        shift = line[:, span] * scale * scale * scale
        scale = jnp.broadcast_to(scale, (LANES, LANES)).T[:, 0:1]
        shift = jnp.broadcast_to(shift, (LANES, LANES)).T[:, 0:1]
        dtgt = own_ref[span, :] + low_ref[span, :].astype(F32) + high_ref[span, :].astype(F32)
        out_ref[span, :] = (dtgt * scale - targets_ref[span, :].astype(F32) * shift).astype(BF16)


def local(hidden, targets, w_proj, mask_counts, mask_pos, negatives):
    shard = lax.axis_index("dp")
    core = (shard % 2).astype(I32).reshape(1)
    half = lax.axis_index("param").astype(I32).reshape(1)
    n_dp = lax.axis_size("dp")
    n_pipe = lax.axis_size("pipe")
    peers = [[2 * (X_CHIPS * z + x) + c for x in range(X_CHIPS) for z in range(Z_CHIPS)] for c in range(2)]
    in_x = [[2 * (X_CHIPS * z + x) + c for x in range(X_CHIPS)] for z in range(Z_CHIPS) for c in range(2)]
    in_z = [[2 * (X_CHIPS * z + x) + c for z in range(Z_CHIPS)] for x in range(X_CHIPS) for c in range(2)]
    swap = [(i, i ^ 1) for i in range(n_dp)]
    upward = [(i, i + 1) for i in range(n_dp - 1)]
    downward = [(i + 1, i) for i in range(n_dp - 1)]
    back = [(i, (i - 1) % n_pipe) for i in range(n_pipe)]
    back_across = [
        (2 * i + a, 2 * ((i - 1) % n_pipe) + 1 - a) for i in range(n_pipe) for a in range(2)
    ]

    (w_blocks,) = call(blocks_body, [((PEERS, PAD, FEATS), BF16)], 0, 1, bytes_accessed=10**6)(w_proj)
    w_own = lax.all_to_all(w_blocks, "dp", 0, 0, axis_index_groups=peers, tiled=True).reshape(HALF, FEATS)
    own_targets = targets[0]
    low = lax.ppermute(own_targets, "dp", upward)
    high = lax.ppermute(own_targets, "dp", downward)
    positions = mask_pos[0, 0] - shard * FRAMES

    frames = jnp.concatenate([mask_pos[0, 0][None, :], negatives[0, 0]], axis=0) - (shard - 1) * FRAMES
    frames = jnp.pad(frames, ((0, LANES - COLUMNS), (0, 0)), constant_values=-1)

    rows_own, rows_other, turned_own, turned_other = call(
        rows_body,
        [((SLOTS, HALF), BF16)] * 2 + [((HALF, SLOTS), BF16)] * 2,
        1, 2, scratch=[pltpu.VMEM((HALF, SLOTS), F32)], flops=2 * 10**9, bytes_accessed=4 * 10**6, vmem=16,
    )(core, positions[:, None], hidden[0])
    turned_got = lax.ppermute(turned_other, "dp", swap)

    packed, times, frames = call(
        index_body, [((SLOTS, WORDS * LANES), I32), ((SLOTS, LANES), F32), ((SLOTS, LANES), I32)], 0, 1,
        scratch=[pltpu.VMEM((2 * WORDS + 2, LANES, SLOTS), I32)], flops=5 * 10**9, bytes_accessed=10**6,
    )(frames)

    window, norms = call(
        window_body, [((WINDOW, FEATS), BF16), ((16, LANES), F32)], 0, 3, flops=10**6, bytes_accessed=3 * 10**6
    )(low, own_targets, high)
    w_own, rows_own, rows_other, turned_own, turned_got, packed, times, frames, window, norms = lax.optimization_barrier(
        (w_own, rows_own, rows_other, turned_own, turned_got, packed, times, frames, window, norms)
    )
    w_other = lax.ppermute(w_own, "dp", swap)

    (part,) = call(
        part_body, [((SLOTS, FEATS), F32)], 0, 2, flops=3 * 10**8, bytes_accessed=2 * 10**6
    )(rows_own, w_own)
    sent, context = call(
        score_body, [((SLOTS + 16, LANES), F32), ((SLOTS, FEATS), F32)], 0, 6,
        scratch=[pltpu.VMEM((SLOTS, WINDOW), F32)], flops=10**9, bytes_accessed=6 * 10**6,
    )(part, rows_other, w_other, window, frames, norms)
    got = lax.ppermute(sent, "param", [(0, 1), (1, 0)])

    dctx, unit, step, along = call(
        slots_body,
        [((SLOTS + 16, FEATS), BF16), ((SLOTS, FEATS), BF16)] + [((SLOTS, LANES), F32)] * 2,
        1, 8,
        scratch=[pltpu.VMEM((SLOTS, LANES), F32)] * 2 + [pltpu.VMEM((SLOTS, WINDOW), BF16)],
        flops=5 * 10**8, bytes_accessed=5 * 10**6,
    )(mask_counts[0], positions[None, :], sent, got, context, frames, times, packed, window)
    dctx_got = lax.ppermute(dctx, "dp", swap)

    (cross,) = call(
        cross_body, [((SLOTS, HALF), BF16)], 1, 3, flops=5 * 10**8, bytes_accessed=2 * 10**6
    )(half, dctx, w_own, w_other)
    cross, dctx_got = lax.optimization_barrier((cross, dctx_got))
    cross = lax.ppermute(cross, ("pipe", "param"), back_across)
    (share,) = call(
        share_body, [((HALF, FEATS), BF16)], 0, 4, flops=5 * 10**8, bytes_accessed=3 * 10**6
    )(turned_own, turned_got, dctx, dctx_got)
    step, share, dctx = lax.optimization_barrier((step, share, dctx))
    same = lax.ppermute(dctx, "pipe", back)
    shares = lax.all_to_all(
        share.reshape(X_CHIPS, HALF // X_CHIPS, FEATS), "dp", 0, 0, axis_index_groups=in_x, tiled=True
    )
    to_low, dtgt, to_high, line = call(
        frames_body,
        [((FRAMES + 16, FEATS), BF16), ((FRAMES, FEATS), F32), ((FRAMES + 16, FEATS), BF16), ((8, FRAMES), F32)],
        0, 4,
        scratch=[pltpu.VMEM((SLOTS, WINDOW), BF16), pltpu.VMEM((8, WINDOW), F32)],
        flops=10**5, bytes_accessed=10**4,
    )(step, along, packed, unit)
    shares, line = lax.optimization_barrier((shares, line))
    (share,) = call(
        merge_body, [((HALF // X_CHIPS, FEATS), BF16)], 0, 1, flops=10**6, bytes_accessed=10**6
    )(shares)
    shares = lax.all_to_all(
        share.reshape(Z_CHIPS, PAD, FEATS), "dp", 0, 0, axis_index_groups=in_z, tiled=True
    )
    from_low = lax.ppermute(to_high, "dp", upward)
    from_high = lax.ppermute(to_low, "dp", downward)


    (token,) = call(
        token_body, [((8, LANES), F32)], 0, 0, flops=15 * 10**9, bytes_accessed=10**5, n_far=2
    )(cross, same)
    (copies,) = call(
        total_body, [((n_pipe, PAD, FEATS), F32)], 0, 1, flops=10**6, bytes_accessed=10**6, n_far=1
    )(shares, token)

    copies, line = lax.optimization_barrier((copies, line))
    pipe_parts = lax.all_to_all(copies, "pipe", 0, 0, tiled=True)
    (upstream,) = call(
        spread_body, [((FRAMES, MODEL // 2), BF16)], 2, 5,
        flops=1 * 10**9, bytes_accessed=4 * 10**6, vmem=16,
    )(core, half, same, cross, w_own, w_other, line)
    (grad_t,) = call(
        targets_body, [((FRAMES, FEATS), BF16)], 0, 7, flops=10**7, bytes_accessed=3 * 10**6
    )(own_targets, dtgt, from_low, from_high, line, sent, got)
    (grad_w,) = call(sum_body, [((BLOCK, FEATS), F32)], 0, 1, flops=10**5, bytes_accessed=10**5)(pipe_parts)
    return (grad_w, upstream[None], grad_t[None])


def solution(mesh):
    return jax.shard_map(
        local,
        mesh=mesh,
        in_specs=(
            P("pipe", "dp", None),
            P("pipe", "dp", "param"),
            P("dp", "param"),
            P("pipe", "dp"),
            P("pipe", "dp", None),
            P("pipe", "dp", None, None),
        ),
        out_specs=(P("dp", "param"), P("pipe", "dp", "param"), P("pipe", "dp", "param")),
        check_vma=False,
    )
```

```python
import jax
import jax.numpy as jnp
from jax import lax
from jax.experimental import pallas as pl
from jax.experimental.pallas import tpu as pltpu
from jax.sharding import PartitionSpec as P

sharpness_divisor = 0.1
loss_multiplier = 32.0
epsilon = 1e-06

F32 = jnp.float32
BF16 = jnp.bfloat16
I32 = jnp.int32

LANES = 128
SLOTS = 256
FRAMES = 512
WINDOW = 3 * FRAMES
TILES = WINDOW // LANES
WORDS = TILES // 4
COLUMNS = 101
SPARE = LANES - 1
GROUP = 64
MODEL = 1920
FEATS = 512
BLOCK = 30
PAD = 32
PEERS = 32
HALF = PEERS * PAD
X_CHIPS = 4
Z_CHIPS = 8
QUARTER = HALF // X_CHIPS // 2


def iota(shape, dim):
    return lax.broadcasted_iota(I32, shape, dim)


def one_hot(hits):
    return jnp.where(hits, 1.0, 0.0).astype(BF16)


def dot(left, right):
    return jnp.dot(left, right, preferred_element_type=F32)


def dot_cols(left, right):
    return lax.dot_general(left, right, (((1,), (1,)), ((), ())), preferred_element_type=F32)


def dot_rows(left, right):
    return lax.dot_general(left, right, (((0,), (0,)), ((), ())), preferred_element_type=F32)


def lookup(table, index):
    return jnp.take_along_axis(table, index, axis=1, mode="promise_in_bounds")


def call(body, outs, n_scalars, n_arrays, scratch=(), flops=0, bytes_accessed=0, vmem=8, n_far=0):
    return pl.pallas_call(
        body,
        out_shape=tuple(jax.ShapeDtypeStruct(shape, dtype) for shape, dtype in outs),
        in_specs=[pl.BlockSpec(memory_space=pltpu.SMEM)] * n_scalars
        + [pl.BlockSpec(memory_space=pltpu.VMEM)] * n_arrays
        + [pl.BlockSpec(memory_space=pl.ANY)] * n_far,
        out_specs=tuple(pl.BlockSpec(memory_space=pltpu.VMEM) for _ in outs),
        scratch_shapes=list(scratch),
        compiler_params=pltpu.CompilerParams(vmem_limit_bytes=vmem * 1024 * 1024),
        cost_estimate=pl.CostEstimate(
            flops=flops, bytes_accessed=bytes_accessed, transcendentals=0
        ),
    )


def blocks_body(w_ref, out_ref):
    block = w_ref[...].astype(F32)
    block = jnp.concatenate([block, jnp.zeros((PAD - BLOCK, FEATS), F32)], axis=0).astype(BF16)
    for i in range(out_ref.shape[0]):
        out_ref[i] = block


def copies_body(rows_ref, out_ref):
    for i in range(out_ref.shape[0]):
        out_ref[i] = rows_ref[...]


def window_body(low_ref, own_ref, high_ref, window_ref, norm_ref):
    norm_ref[...] = jnp.zeros((16, LANES), F32)
    for part, ref in enumerate((low_ref, own_ref, high_ref)):
        for k in range(FRAMES // LANES):
            frames = ref[LANES * k : LANES * (k + 1), :]
            at = part * FRAMES + LANES * k
            window_ref[at : at + LANES, :] = frames
            square = frames.astype(F32)
            square = square * square
            partial = sum(square[:, LANES * i : LANES * (i + 1)] for i in range(FEATS // LANES))
            t = at // LANES
            norm_ref[t : t + 1, :] = jnp.sum(partial.T, axis=0, keepdims=True)


def rows_body(core_ref, pos_ref, hidden_ref, own_ref, other_ref, own_t_ref, other_t_ref, turn_ref):
    chosen = one_hot(pos_ref[...] == iota((SLOTS, FRAMES), 1))
    rows = dot(chosen, hidden_ref[...]).astype(BF16)
    core = core_ref[0]
    step = 256
    for parity, straight, turned in ((core, own_ref, own_t_ref), (1 - core, other_ref, other_t_ref)):
        for k in range(HALF // step):
            low = (2 * BLOCK * step // PAD * k) // LANES * LANES
            wide = min(MODEL, low + 640) - low
            q = iota((step, wide), 0) + step * k
            wanted = BLOCK * (2 * (q >> 5) + parity) + (q & 31)
            spread = one_hot((wanted == iota((step, wide), 1) + low) & ((q & 31) < BLOCK))
            piece = dot_cols(spread, rows[:, low : low + wide])
            for i in range(step // PAD):
                z, x = divmod(step // PAD * k + i, X_CHIPS)
                at = PAD * (x * Z_CHIPS + z)
                turn_ref[at : at + PAD, :] = piece[PAD * i : PAD * (i + 1), :]
        turned[...] = turn_ref[...].astype(BF16)
        for g in range(HALF // LANES):
            span = slice(LANES * g, LANES * (g + 1))
            straight[:, span] = turn_ref[span, :].T.astype(BF16)


def index_body(named_ref, packed_ref, times_ref, frame_ref, words_ref):
    depth = 32
    here_at, times_at = WORDS, WORDS + 1
    for side in range(SLOTS // LANES):
        across = slice(LANES * side, LANES * (side + 1))

        def prepare(i, carry):
            rows = pl.ds(pl.multiple_of(i * depth, depth), depth)
            part = named_ref[rows, across]
            times = jnp.zeros((depth, LANES), I32)
            first = jnp.full((depth, LANES), SPARE, I32)
            for c in reversed(range(COLUMNS)):
                same = part == jnp.broadcast_to(named_ref[c : c + 1, across], (depth, LANES))
                times = times + jnp.where(same, 1, 0)
                first = jnp.where(same, c, first)
            mine = iota((depth, LANES), 0) + i * depth
            tile = part >> 7
            value = jnp.where((first == mine) & (mine < COLUMNS), (SPARE - mine) << ((tile & 3) * 8), 0)
            for w in range(WORDS):
                words_ref[w, rows, across] = jnp.where((tile >> 2) == w, value, 0)
            words_ref[here_at, rows, across] = part & 127
            words_ref[times_at, rows, across] = times
            return carry

        def pack(i, carry):
            rows = pl.ds(pl.multiple_of(i * depth, depth), depth)
            place = iota((depth, LANES), 0) + i * depth
            packed = [jnp.zeros((depth, LANES), I32) for _ in range(WORDS)]
            for c in range(COLUMNS):
                here = place == jnp.broadcast_to(words_ref[here_at, c : c + 1, across], (depth, LANES))
                for w in range(WORDS):
                    word = jnp.broadcast_to(words_ref[w, c : c + 1, across], (depth, LANES))
                    packed[w] = packed[w] + jnp.where(here, word, 0)
            for w in range(WORDS):
                words_ref[times_at + 1 + w, rows, across] = packed[w]
            return carry

        lax.fori_loop(0, LANES // depth, prepare, 0)
        lax.fori_loop(0, LANES // depth, pack, 0)
        times_ref[across, :] = words_ref[times_at, :, across].T.astype(F32)
        frame_ref[across, :] = named_ref[:, across].T
        for w in range(WORDS):
            packed_ref[across, LANES * w : LANES * (w + 1)] = words_ref[times_at + 1 + w, :, across].T


def columns_of(packed_ref, rows):
    for w in range(WORDS):
        word = packed_ref[rows, LANES * w : LANES * (w + 1)]
        for k in range(4):
            yield 4 * w + k, SPARE - ((word >> (8 * k)) & 127)


def part_body(rows_ref, w_ref, out_ref):
    out_ref[...] = dot(rows_ref[...], w_ref[...])


def score_body(part_ref, other_ref, w_other_ref, window_ref, frame_ref, norm_ref, sent_ref, context_ref, table_ref):
    context = part_ref[...] + dot(other_ref[...], w_other_ref[...])
    context_ref[...] = context
    table_ref[...] = dot_cols(context.astype(BF16), window_ref[...])
    sent_ref[0:SLOTS, :] = jnp.broadcast_to(
        jnp.sum(context * context, axis=1, keepdims=True), (SLOTS, LANES)
    )
    sent_ref[SLOTS : SLOTS + 16, :] = norm_ref[...]
    lane = iota((GROUP, LANES), 1)

    def group(g, carry):
        rows = pl.ds(pl.multiple_of(g * GROUP, GROUP), GROUP)
        frame = frame_ref[rows, :]
        tile, place = frame >> 7, frame & 127
        picked = jnp.where(lane == COLUMNS, sent_ref[rows, :], 0.0)
        for t in range(TILES):
            found = lookup(table_ref[rows, LANES * t : LANES * (t + 1)], place)
            picked = jnp.where((tile == t) & (lane < COLUMNS), found, picked)
        sent_ref[rows, :] = picked
        return carry

    lax.fori_loop(0, SLOTS // GROUP, group, 0)


def slots_body(
    count_ref, place_ref, sent_ref, got_ref, context_ref, frame_ref, times_ref, packed_ref, window_ref,
    dctx_ref, unit_ref, step_ref, along_ref, inverse_ref, shift_ref, scores_ref,
):
    inv_tgt = 1.0 / jnp.sqrt(
        sent_ref[SLOTS : SLOTS + 16, :] + got_ref[SLOTS : SLOTS + 16, :] + epsilon
    )
    lane = iota((GROUP, LANES), 1)
    named = lane < COLUMNS
    count = count_ref[0]

    def group(g, carry):
        rows = pl.ds(pl.multiple_of(g * GROUP, GROUP), GROUP)
        raw = sent_ref[rows, :] + got_ref[rows, :]
        inverse = 1.0 / jnp.sqrt(raw[:, COLUMNS : COLUMNS + 1] + epsilon)
        frame = frame_ref[rows, :]
        tile, place = frame >> 7, frame & 127
        scale = jnp.zeros((GROUP, LANES), F32)
        for t in range(TILES):
            line = jnp.broadcast_to(inv_tgt[t : t + 1, :], (GROUP, LANES))
            scale = jnp.where(tile == t, lookup(line, place), scale)
        logits = raw * inverse * scale / sharpness_divisor
        expon = jnp.where(named, jnp.exp(jnp.where(named, logits, 0.0)), 0.0)
        probs = expon / jnp.sum(expon, axis=1, keepdims=True)
        live = iota((GROUP, LANES), 0) + g * GROUP < count
        first = jnp.where(lane == 0, 1.0, 0.0)
        step = jnp.where(live & named, loss_multiplier * (probs - first) / sharpness_divisor, 0.0)
        times = jnp.maximum(times_ref[rows, :], 1.0)
        step = step * times
        weight = (step * scale).astype(BF16).astype(F32)
        along = jnp.sum(jnp.where(named, weight * raw / times, 0.0), axis=1, keepdims=True)
        step_ref[rows, :] = step
        along_ref[rows, :] = jnp.where(named, step.astype(BF16).astype(F32) * raw * inverse, 0.0)
        inverse_ref[rows, :] = jnp.broadcast_to(inverse, (GROUP, LANES))
        shift_ref[rows, :] = jnp.broadcast_to(along * inverse * inverse * inverse, (GROUP, LANES))
        for t, column in columns_of(packed_ref, rows):
            scores_ref[rows, LANES * t : LANES * (t + 1)] = lookup(weight, column).astype(BF16)
        return carry

    lax.fori_loop(0, SLOTS // GROUP, group, 0)
    context = context_ref[...]
    inverse = inverse_ref[:, 0:1]
    dunit = dot(scores_ref[...], window_ref[...])
    dctx_ref[0:SLOTS, :] = (dunit * inverse - context * shift_ref[:, 0:1]).astype(BF16)
    places = jnp.broadcast_to(place_ref[...], (16, SLOTS))
    parts = jnp.where(iota((16, SLOTS), 0) == 0, places >> 4, places & 15)
    dctx_ref[SLOTS : SLOTS + 16, :] = jnp.zeros((16, FEATS), BF16)
    dctx_ref[SLOTS : SLOTS + 16, 0:SLOTS] = parts.astype(F32).astype(BF16)
    unit_ref[...] = (context * inverse).astype(BF16)


def frames_body(step_ref, along_ref, packed_ref, unit_ref, low_ref, own_ref, high_ref, line_ref, scores_ref, sums_ref):
    sums_ref[...] = jnp.zeros((8, WINDOW), F32)

    def group(g, carry):
        rows = pl.ds(pl.multiple_of(g * GROUP, GROUP), GROUP)
        step = step_ref[rows, :]
        along = along_ref[rows, :]
        for t, column in columns_of(packed_ref, rows):
            span = slice(LANES * t, LANES * (t + 1))
            scores_ref[rows, span] = lookup(step, column).astype(BF16)
            sums_ref[:, span] += jnp.sum(lookup(along, column).reshape(GROUP // 8, 8, LANES), axis=0)
        return carry

    lax.fori_loop(0, SLOTS // GROUP, group, 0)
    line = jnp.sum(sums_ref[...], axis=0, keepdims=True)
    line_ref[...] = jnp.broadcast_to(line[:, FRAMES : 2 * FRAMES], (8, FRAMES))
    row = iota((16, FRAMES), 0)
    for part, ref in ((0, low_ref), (1, own_ref), (2, high_ref)):
        span = slice(FRAMES * part, FRAMES * (part + 1))
        ref[0:FRAMES, :] = dot_rows(scores_ref[:, span], unit_ref[...]).astype(ref.dtype)
        if part != 1:
            left = jnp.broadcast_to(line[:, span], (16, FRAMES))
            first = left.astype(BF16).astype(F32)
            second = (left - first).astype(BF16).astype(F32)
            third = left - first - second
            ref[FRAMES : FRAMES + 16, :] = jnp.where(
                row == 0, first, jnp.where(row == 1, second, jnp.where(row == 2, third, 0.0))
            ).astype(BF16)


def share_body(turned_own_ref, turned_got_ref, own_ref, got_ref, out_ref):
    own = dot(turned_own_ref[...], own_ref[0:SLOTS, :])
    out_ref[...] = (own + dot(turned_got_ref[...], got_ref[0:SLOTS, :])).astype(BF16)


def merge_body(parts_ref, out_ref):
    out_ref[...] = jnp.sum(parts_ref[...].astype(F32), axis=0).astype(BF16)


def token_body(cross_ref, same_ref, out_ref):
    out_ref[...] = jnp.zeros((8, LANES), F32)


def total_body(parts_ref, token_ref, out_ref):
    total = jnp.sum(parts_ref[...].astype(F32), axis=0)
    for i in range(out_ref.shape[0]):
        out_ref[i] = total


def sum_body(parts_ref, out_ref):
    out_ref[...] = jnp.sum(parts_ref[...], axis=0)[0:BLOCK, :]


def half_of(w_ref, half):
    return jnp.concatenate(
        [
            w_ref[pl.ds(pl.multiple_of(2 * QUARTER * x + half * QUARTER, QUARTER), QUARTER), :]
            for x in range(X_CHIPS)
        ],
        axis=0,
    )


def cross_body(half_ref, dctx_ref, w_own_ref, w_other_ref, cross_ref):
    half = 1 - half_ref[0]
    dctx = dctx_ref[0:SLOTS, :]
    cross_ref[:, 0 : HALF // 2] = dot_cols(dctx, half_of(w_own_ref, half)).astype(BF16)
    cross_ref[:, HALF // 2 : HALF] = dot_cols(dctx, half_of(w_other_ref, half)).astype(BF16)


def spread_body(core_ref, half_ref, same_ref, cross_ref, w_own_ref, w_other_ref, line_ref, out_ref):
    core = core_ref[0]
    dctx = same_ref[0:SLOTS, :]
    parts = same_ref[SLOTS : SLOTS + 16, 0:SLOTS].astype(F32)
    places = (parts[0:1, :] * 16.0 + parts[1:2, :]).astype(I32)
    placed = one_hot(iota((FRAMES, SLOTS), 0) == places)
    shape = (HALF // 2, MODEL // 2)
    rows = jnp.zeros((SLOTS, MODEL // 2), F32)
    for side, (parity, w_ref) in enumerate(((core, w_own_ref), (1 - core, w_other_ref))):
        span = slice(HALF // 2 * side, HALF // 2 * (side + 1))
        drows = (dot_cols(dctx, half_of(w_ref, half_ref[0])) + cross_ref[:, span].astype(F32)).astype(BF16)
        q = iota(shape, 0)
        block = 2 * (X_CHIPS * ((q >> 5) & (Z_CHIPS // 2 - 1)) + (q >> 7)) + parity
        unpad = one_hot((BLOCK * block + (q & 31) == iota(shape, 1)) & ((q & 31) < BLOCK))
        rows = rows + dot(drows, unpad)
    out_ref[...] = dot(placed, rows.astype(BF16)).astype(BF16)


def targets_body(targets_ref, own_ref, low_ref, high_ref, line_ref, sent_ref, got_ref, out_ref):
    tail = slice(FRAMES, FRAMES + 16)
    line = line_ref[0:1, :] + jnp.sum(
        low_ref[tail, :].astype(F32) + high_ref[tail, :].astype(F32), axis=0, keepdims=True
    )
    inv_tgt = 1.0 / jnp.sqrt(
        sent_ref[SLOTS : SLOTS + 16, :] + got_ref[SLOTS : SLOTS + 16, :] + epsilon
    )
    for t in range(FRAMES // LANES):
        span = slice(LANES * t, LANES * (t + 1))
        scale = inv_tgt[TILES // 3 + t : TILES // 3 + t + 1, :]
        shift = line[:, span] * scale * scale * scale
        scale = jnp.broadcast_to(scale, (LANES, LANES)).T[:, 0:1]
        shift = jnp.broadcast_to(shift, (LANES, LANES)).T[:, 0:1]
        dtgt = own_ref[span, :] + low_ref[span, :].astype(F32) + high_ref[span, :].astype(F32)
        out_ref[span, :] = (dtgt * scale - targets_ref[span, :].astype(F32) * shift).astype(BF16)


def local(hidden, targets, w_proj, mask_counts, mask_pos, negatives):
    shard = lax.axis_index("dp")
    core = (shard % 2).astype(I32).reshape(1)
    half = lax.axis_index("param").astype(I32).reshape(1)
    n_dp = lax.axis_size("dp")
    n_pipe = lax.axis_size("pipe")
    peers = [[2 * (X_CHIPS * z + x) + c for x in range(X_CHIPS) for z in range(Z_CHIPS)] for c in range(2)]
    in_x = [[2 * (X_CHIPS * z + x) + c for x in range(X_CHIPS)] for z in range(Z_CHIPS) for c in range(2)]
    in_z = [[2 * (X_CHIPS * z + x) + c for z in range(Z_CHIPS)] for x in range(X_CHIPS) for c in range(2)]
    swap = [(i, i ^ 1) for i in range(n_dp)]
    upward = [(i, i + 1) for i in range(n_dp - 1)]
    downward = [(i + 1, i) for i in range(n_dp - 1)]
    back = [(i, (i - 1) % n_pipe) for i in range(n_pipe)]
    back_across = [
        (2 * i + a, 2 * ((i - 1) % n_pipe) + 1 - a) for i in range(n_pipe) for a in range(2)
    ]

    (w_blocks,) = call(blocks_body, [((Z_CHIPS, PAD, FEATS), BF16)], 0, 1, bytes_accessed=10**5)(w_proj)
    w_blocks = lax.all_to_all(w_blocks, "dp", 0, 0, axis_index_groups=in_z, tiled=True)
    (w_blocks,) = call(
        copies_body, [((X_CHIPS, HALF // X_CHIPS, FEATS), BF16)], 0, 1, bytes_accessed=10**6
    )(w_blocks.reshape(HALF // X_CHIPS, FEATS))
    w_own = lax.all_to_all(w_blocks, "dp", 0, 0, axis_index_groups=in_x, tiled=True).reshape(HALF, FEATS)

    own_targets = targets[0]
    low = lax.ppermute(own_targets, "dp", upward)
    high = lax.ppermute(own_targets, "dp", downward)
    positions = mask_pos[0, 0] - shard * FRAMES

    frames = jnp.concatenate([mask_pos[0, 0][None, :], negatives[0, 0]], axis=0) - (shard - 1) * FRAMES
    frames = jnp.pad(frames, ((0, LANES - COLUMNS), (0, 0)), constant_values=-1)

    rows_own, rows_other, turned_own, turned_other = call(
        rows_body,
        [((SLOTS, HALF), BF16)] * 2 + [((HALF, SLOTS), BF16)] * 2,
        1, 2, scratch=[pltpu.VMEM((HALF, SLOTS), F32)], flops=2 * 10**9, bytes_accessed=4 * 10**6, vmem=16,
    )(core, positions[:, None], hidden[0])
    turned_got = lax.ppermute(turned_other, "dp", swap)

    packed, times, frames = call(
        index_body, [((SLOTS, WORDS * LANES), I32), ((SLOTS, LANES), F32), ((SLOTS, LANES), I32)], 0, 1,
        scratch=[pltpu.VMEM((2 * WORDS + 2, LANES, SLOTS), I32)], flops=5 * 10**9, bytes_accessed=10**6,
    )(frames)

    window, norms = call(
        window_body, [((WINDOW, FEATS), BF16), ((16, LANES), F32)], 0, 3, flops=10**6, bytes_accessed=3 * 10**6
    )(low, own_targets, high)
    w_own, rows_own, rows_other, turned_own, turned_got, packed, times, frames, window, norms = lax.optimization_barrier(
        (w_own, rows_own, rows_other, turned_own, turned_got, packed, times, frames, window, norms)
    )
    w_other = lax.ppermute(w_own, "dp", swap)

    (part,) = call(
        part_body, [((SLOTS, FEATS), F32)], 0, 2, flops=3 * 10**8, bytes_accessed=2 * 10**6
    )(rows_own, w_own)
    sent, context = call(
        score_body, [((SLOTS + 16, LANES), F32), ((SLOTS, FEATS), F32)], 0, 6,
        scratch=[pltpu.VMEM((SLOTS, WINDOW), F32)], flops=10**9, bytes_accessed=6 * 10**6,
    )(part, rows_other, w_other, window, frames, norms)
    got = lax.ppermute(sent, "param", [(0, 1), (1, 0)])

    dctx, unit, step, along = call(
        slots_body,
        [((SLOTS + 16, FEATS), BF16), ((SLOTS, FEATS), BF16)] + [((SLOTS, LANES), F32)] * 2,
        1, 8,
        scratch=[pltpu.VMEM((SLOTS, LANES), F32)] * 2 + [pltpu.VMEM((SLOTS, WINDOW), BF16)],
        flops=5 * 10**8, bytes_accessed=5 * 10**6,
    )(mask_counts[0], positions[None, :], sent, got, context, frames, times, packed, window)
    dctx_got = lax.ppermute(dctx, "dp", swap)

    (cross,) = call(
        cross_body, [((SLOTS, HALF), BF16)], 1, 3, flops=5 * 10**8, bytes_accessed=2 * 10**6
    )(half, dctx, w_own, w_other)
    cross, dctx_got = lax.optimization_barrier((cross, dctx_got))
    cross = lax.ppermute(cross, ("pipe", "param"), back_across)
    (share,) = call(
        share_body, [((HALF, FEATS), BF16)], 0, 4, flops=5 * 10**8, bytes_accessed=3 * 10**6
    )(turned_own, turned_got, dctx, dctx_got)
    step, share, dctx = lax.optimization_barrier((step, share, dctx))
    same = lax.ppermute(dctx, "pipe", back)
    shares = lax.all_to_all(
        share.reshape(X_CHIPS, HALF // X_CHIPS, FEATS), "dp", 0, 0, axis_index_groups=in_x, tiled=True
    )
    to_low, dtgt, to_high, line = call(
        frames_body,
        [((FRAMES + 16, FEATS), BF16), ((FRAMES, FEATS), F32), ((FRAMES + 16, FEATS), BF16), ((8, FRAMES), F32)],
        0, 4,
        scratch=[pltpu.VMEM((SLOTS, WINDOW), BF16), pltpu.VMEM((8, WINDOW), F32)],
        flops=10**5, bytes_accessed=10**4,
    )(step, along, packed, unit)
    shares, line = lax.optimization_barrier((shares, line))
    (share,) = call(
        merge_body, [((HALF // X_CHIPS, FEATS), BF16)], 0, 1, flops=10**6, bytes_accessed=10**6
    )(shares)
    shares = lax.all_to_all(
        share.reshape(Z_CHIPS, PAD, FEATS), "dp", 0, 0, axis_index_groups=in_z, tiled=True
    )
    from_low = lax.ppermute(to_high, "dp", upward)
    from_high = lax.ppermute(to_low, "dp", downward)


    (token,) = call(
        token_body, [((8, LANES), F32)], 0, 0, flops=15 * 10**9, bytes_accessed=10**5, n_far=2
    )(cross, same)
    (copies,) = call(
        total_body, [((n_pipe, PAD, FEATS), F32)], 0, 1, flops=10**6, bytes_accessed=10**6, n_far=1
    )(shares, token)

    copies, line = lax.optimization_barrier((copies, line))
    pipe_parts = lax.all_to_all(copies, "pipe", 0, 0, tiled=True)
    (upstream,) = call(
        spread_body, [((FRAMES, MODEL // 2), BF16)], 2, 5,
        flops=1 * 10**9, bytes_accessed=4 * 10**6, vmem=16,
    )(core, half, same, cross, w_own, w_other, line)
    (grad_t,) = call(
        targets_body, [((FRAMES, FEATS), BF16)], 0, 7, flops=10**7, bytes_accessed=3 * 10**6
    )(own_targets, dtgt, from_low, from_high, line, sent, got)
    (grad_w,) = call(sum_body, [((BLOCK, FEATS), F32)], 0, 1, flops=10**5, bytes_accessed=10**5)(pipe_parts)
    return (grad_w, upstream[None], grad_t[None])


def solution(mesh):
    return jax.shard_map(
        local,
        mesh=mesh,
        in_specs=(
            P("pipe", "dp", None),
            P("pipe", "dp", "param"),
            P("dp", "param"),
            P("pipe", "dp"),
            P("pipe", "dp", None),
            P("pipe", "dp", None, None),
        ),
        out_specs=(P("dp", "param"), P("pipe", "dp", "param"), P("pipe", "dp", "param")),
        check_vma=False,
    )
```

```python
import jax
import jax.numpy as jnp
from jax import lax
from jax.experimental import pallas as pl
from jax.experimental.pallas import tpu as pltpu
from jax.sharding import PartitionSpec as P

sharpness_divisor = 0.1
loss_multiplier = 32.0
epsilon = 1e-06

F32 = jnp.float32
BF16 = jnp.bfloat16
I32 = jnp.int32

LANES = 128
SLOTS = 256
FRAMES = 512
WINDOW = 3 * FRAMES
TILES = WINDOW // LANES
WORDS = TILES // 4
COLUMNS = 101
SPARE = LANES - 1
GROUP = 64
MODEL = 1920
FEATS = 512
BLOCK = 30
PAD = 32
PEERS = 32
HALF = PEERS * PAD
X_CHIPS = 4
Z_CHIPS = 8
QUARTER = HALF // X_CHIPS // 2


def iota(shape, dim):
    return lax.broadcasted_iota(I32, shape, dim)


def one_hot(hits):
    return jnp.where(hits, 1.0, 0.0).astype(BF16)


def dot(left, right):
    return jnp.dot(left, right, preferred_element_type=F32)


def dot_cols(left, right):
    return lax.dot_general(left, right, (((1,), (1,)), ((), ())), preferred_element_type=F32)


def dot_rows(left, right):
    return lax.dot_general(left, right, (((0,), (0,)), ((), ())), preferred_element_type=F32)


def lookup(table, index):
    return jnp.take_along_axis(table, index, axis=1, mode="promise_in_bounds")


def call(body, outs, n_scalars, n_arrays, scratch=(), flops=0, bytes_accessed=0, vmem=8, n_far=0):
    return pl.pallas_call(
        body,
        out_shape=tuple(jax.ShapeDtypeStruct(shape, dtype) for shape, dtype in outs),
        in_specs=[pl.BlockSpec(memory_space=pltpu.SMEM)] * n_scalars
        + [pl.BlockSpec(memory_space=pltpu.VMEM)] * n_arrays
        + [pl.BlockSpec(memory_space=pl.ANY)] * n_far,
        out_specs=tuple(pl.BlockSpec(memory_space=pltpu.VMEM) for _ in outs),
        scratch_shapes=list(scratch),
        compiler_params=pltpu.CompilerParams(vmem_limit_bytes=vmem * 1024 * 1024),
        cost_estimate=pl.CostEstimate(
            flops=flops, bytes_accessed=bytes_accessed, transcendentals=0
        ),
    )


def blocks_body(w_ref, out_ref):
    block = w_ref[...].astype(F32)
    block = jnp.concatenate([block, jnp.zeros((PAD - BLOCK, FEATS), F32)], axis=0).astype(BF16)
    for i in range(out_ref.shape[0]):
        out_ref[i] = block


def copies_body(rows_ref, out_ref):
    for i in range(out_ref.shape[0]):
        out_ref[i] = rows_ref[...]


def window_body(low_ref, own_ref, high_ref, window_ref, norm_ref):
    norm_ref[...] = jnp.zeros((16, LANES), F32)
    for part, ref in enumerate((low_ref, own_ref, high_ref)):
        for k in range(FRAMES // LANES):
            frames = ref[LANES * k : LANES * (k + 1), :]
            at = part * FRAMES + LANES * k
            window_ref[at : at + LANES, :] = frames
            square = frames.astype(F32)
            square = square * square
            partial = sum(square[:, LANES * i : LANES * (i + 1)] for i in range(FEATS // LANES))
            t = at // LANES
            norm_ref[t : t + 1, :] = jnp.sum(partial.T, axis=0, keepdims=True)


def rows_body(core_ref, pos_ref, hidden_ref, own_ref, other_ref, own_t_ref, other_t_ref, turn_ref):
    chosen = one_hot(pos_ref[...] == iota((SLOTS, FRAMES), 1))
    rows = dot(chosen, hidden_ref[...]).astype(BF16)
    core = core_ref[0]
    step = 256
    for parity, straight, turned in ((core, own_ref, own_t_ref), (1 - core, other_ref, other_t_ref)):
        for k in range(HALF // step):
            low = (2 * BLOCK * step // PAD * k) // LANES * LANES
            wide = min(MODEL, low + 640) - low
            q = iota((step, wide), 0) + step * k
            wanted = BLOCK * (2 * (q >> 5) + parity) + (q & 31)
            spread = one_hot((wanted == iota((step, wide), 1) + low) & ((q & 31) < BLOCK))
            piece = dot_cols(spread, rows[:, low : low + wide])
            for i in range(step // PAD):
                z, x = divmod(step // PAD * k + i, X_CHIPS)
                at = PAD * (x * Z_CHIPS + z)
                turn_ref[at : at + PAD, :] = piece[PAD * i : PAD * (i + 1), :]
        turned[...] = turn_ref[...].astype(BF16)
        for g in range(HALF // LANES):
            span = slice(LANES * g, LANES * (g + 1))
            straight[:, span] = turn_ref[span, :].T.astype(BF16)


def index_body(named_ref, packed_ref, times_ref, frame_ref, words_ref):
    depth = 32
    here_at, times_at = WORDS, WORDS + 1
    for side in range(SLOTS // LANES):
        across = slice(LANES * side, LANES * (side + 1))

        def prepare(i, carry):
            rows = pl.ds(pl.multiple_of(i * depth, depth), depth)
            part = named_ref[rows, across]
            times = jnp.zeros((depth, LANES), I32)
            first = jnp.full((depth, LANES), SPARE, I32)
            for c in reversed(range(COLUMNS)):
                same = part == jnp.broadcast_to(named_ref[c : c + 1, across], (depth, LANES))
                times = times + jnp.where(same, 1, 0)
                first = jnp.where(same, c, first)
            mine = iota((depth, LANES), 0) + i * depth
            tile = part >> 7
            value = jnp.where((first == mine) & (mine < COLUMNS), (SPARE - mine) << ((tile & 3) * 8), 0)
            for w in range(WORDS):
                words_ref[w, rows, across] = jnp.where((tile >> 2) == w, value, 0)
            words_ref[here_at, rows, across] = part & 127
            words_ref[times_at, rows, across] = times
            return carry

        def pack(i, carry):
            rows = pl.ds(pl.multiple_of(i * depth, depth), depth)
            place = iota((depth, LANES), 0) + i * depth
            packed = [jnp.zeros((depth, LANES), I32) for _ in range(WORDS)]
            for c in range(COLUMNS):
                here = place == jnp.broadcast_to(words_ref[here_at, c : c + 1, across], (depth, LANES))
                for w in range(WORDS):
                    word = jnp.broadcast_to(words_ref[w, c : c + 1, across], (depth, LANES))
                    packed[w] = packed[w] + jnp.where(here, word, 0)
            for w in range(WORDS):
                words_ref[times_at + 1 + w, rows, across] = packed[w]
            return carry

        lax.fori_loop(0, LANES // depth, prepare, 0)
        lax.fori_loop(0, LANES // depth, pack, 0)
        times_ref[across, :] = words_ref[times_at, :, across].T.astype(F32)
        frame_ref[across, :] = named_ref[:, across].T
        for w in range(WORDS):
            packed_ref[across, LANES * w : LANES * (w + 1)] = words_ref[times_at + 1 + w, :, across].T


def columns_of(packed_ref, rows):
    for w in range(WORDS):
        word = packed_ref[rows, LANES * w : LANES * (w + 1)]
        for k in range(4):
            yield 4 * w + k, SPARE - ((word >> (8 * k)) & 127)


def part_body(rows_ref, w_ref, out_ref):
    out_ref[...] = dot(rows_ref[...], w_ref[...])


def score_body(part_ref, other_ref, w_other_ref, window_ref, frame_ref, norm_ref, sent_ref, context_ref, table_ref):
    context = part_ref[...] + dot(other_ref[...], w_other_ref[...])
    context_ref[...] = context
    table_ref[...] = dot_cols(context.astype(BF16), window_ref[...])
    sent_ref[0:SLOTS, :] = jnp.broadcast_to(
        jnp.sum(context * context, axis=1, keepdims=True), (SLOTS, LANES)
    )
    sent_ref[SLOTS : SLOTS + 16, :] = norm_ref[...]
    lane = iota((GROUP, LANES), 1)

    def group(g, carry):
        rows = pl.ds(pl.multiple_of(g * GROUP, GROUP), GROUP)
        frame = frame_ref[rows, :]
        tile, place = frame >> 7, frame & 127
        picked = jnp.where(lane == COLUMNS, sent_ref[rows, :], 0.0)
        for t in range(TILES):
            found = lookup(table_ref[rows, LANES * t : LANES * (t + 1)], place)
            picked = jnp.where((tile == t) & (lane < COLUMNS), found, picked)
        sent_ref[rows, :] = picked
        return carry

    lax.fori_loop(0, SLOTS // GROUP, group, 0)


def slots_body(
    count_ref, place_ref, sent_ref, got_ref, context_ref, frame_ref, times_ref, packed_ref, window_ref,
    dctx_ref, unit_ref, pair_ref, inverse_ref, shift_ref, scores_ref,
):
    inv_tgt = 1.0 / jnp.sqrt(
        sent_ref[SLOTS : SLOTS + 16, :] + got_ref[SLOTS : SLOTS + 16, :] + epsilon
    )
    lane = iota((GROUP, LANES), 1)
    named = lane < COLUMNS
    count = count_ref[0]

    def group(g, carry):
        rows = pl.ds(pl.multiple_of(g * GROUP, GROUP), GROUP)
        raw = sent_ref[rows, :] + got_ref[rows, :]
        inverse = 1.0 / jnp.sqrt(raw[:, COLUMNS : COLUMNS + 1] + epsilon)
        frame = frame_ref[rows, :]
        tile, place = frame >> 7, frame & 127
        scale = jnp.zeros((GROUP, LANES), F32)
        for t in range(TILES):
            line = jnp.broadcast_to(inv_tgt[t : t + 1, :], (GROUP, LANES))
            scale = jnp.where(tile == t, lookup(line, place), scale)
        logits = raw * inverse * scale / sharpness_divisor
        expon = jnp.where(named, jnp.exp(jnp.where(named, logits, 0.0)), 0.0)
        probs = expon / jnp.sum(expon, axis=1, keepdims=True)
        live = iota((GROUP, LANES), 0) + g * GROUP < count
        first = jnp.where(lane == 0, 1.0, 0.0)
        step = jnp.where(live & named, loss_multiplier * (probs - first) / sharpness_divisor, 0.0)
        times = jnp.maximum(times_ref[rows, :], 1.0)
        step = step * times
        weight = (step * scale).astype(BF16).astype(F32)
        along = jnp.sum(jnp.where(named, weight * raw / times, 0.0), axis=1, keepdims=True)
        pair_ref[rows, 0:LANES] = step
        pair_ref[rows, LANES : 2 * LANES] = jnp.where(named, step.astype(BF16).astype(F32) * raw * inverse, 0.0)
        inverse_ref[rows, :] = jnp.broadcast_to(inverse, (GROUP, LANES))
        shift_ref[rows, :] = jnp.broadcast_to(along * inverse * inverse * inverse, (GROUP, LANES))
        for t, column in columns_of(packed_ref, rows):
            scores_ref[rows, LANES * t : LANES * (t + 1)] = lookup(weight, column).astype(BF16)
        return carry

    lax.fori_loop(0, SLOTS // GROUP, group, 0)
    context = context_ref[...]
    inverse = inverse_ref[:, 0:1]
    dunit = dot(scores_ref[...], window_ref[...])
    dctx_ref[0:SLOTS, :] = (dunit * inverse - context * shift_ref[:, 0:1]).astype(BF16)
    places = jnp.broadcast_to(place_ref[...], (16, SLOTS))
    parts = jnp.where(iota((16, SLOTS), 0) == 0, places >> 4, places & 15)
    dctx_ref[SLOTS : SLOTS + 16, :] = jnp.zeros((16, FEATS), BF16)
    dctx_ref[SLOTS : SLOTS + 16, 0:SLOTS] = parts.astype(F32).astype(BF16)
    unit_ref[...] = (context * inverse).astype(BF16)


def frames_body(pair_ref, packed_ref, unit_ref, low_ref, own_ref, high_ref, line_ref, scores_ref, sums_ref):
    sums_ref[...] = jnp.zeros((8, WINDOW), F32)

    def group(g, carry):
        rows = pl.ds(pl.multiple_of(g * GROUP, GROUP), GROUP)
        step = pair_ref[rows, 0:LANES]
        along = pair_ref[rows, LANES : 2 * LANES]
        for t, column in columns_of(packed_ref, rows):
            span = slice(LANES * t, LANES * (t + 1))
            scores_ref[rows, span] = lookup(step, column).astype(BF16)
            sums_ref[:, span] += jnp.sum(lookup(along, column).reshape(GROUP // 8, 8, LANES), axis=0)
        return carry

    lax.fori_loop(0, SLOTS // GROUP, group, 0)
    line = jnp.sum(sums_ref[...], axis=0, keepdims=True)
    line_ref[...] = jnp.broadcast_to(line[:, FRAMES : 2 * FRAMES], (8, FRAMES))
    row = iota((16, FRAMES), 0)
    for part, ref in ((0, low_ref), (1, own_ref), (2, high_ref)):
        span = slice(FRAMES * part, FRAMES * (part + 1))
        ref[0:FRAMES, :] = dot_rows(scores_ref[:, span], unit_ref[...]).astype(ref.dtype)
        if part != 1:
            left = jnp.broadcast_to(line[:, span], (16, FRAMES))
            first = left.astype(BF16).astype(F32)
            second = (left - first).astype(BF16).astype(F32)
            third = left - first - second
            ref[FRAMES : FRAMES + 16, :] = jnp.where(
                row == 0, first, jnp.where(row == 1, second, jnp.where(row == 2, third, 0.0))
            ).astype(BF16)


def share_body(turned_own_ref, turned_got_ref, own_ref, got_ref, out_ref):
    own = dot(turned_own_ref[...], own_ref[0:SLOTS, :])
    out_ref[...] = (own + dot(turned_got_ref[...], got_ref[0:SLOTS, :])).astype(BF16)


def merge_body(parts_ref, out_ref):
    out_ref[...] = jnp.sum(parts_ref[...].astype(F32), axis=0).astype(BF16)


def token_body(cross_ref, same_ref, out_ref):
    out_ref[...] = jnp.zeros((8, LANES), F32)


def total_body(parts_ref, token_ref, out_ref):
    total = jnp.sum(parts_ref[...].astype(F32), axis=0)
    for i in range(out_ref.shape[0]):
        out_ref[i] = total


def sum_body(parts_ref, out_ref):
    out_ref[...] = jnp.sum(parts_ref[...], axis=0)[0:BLOCK, :]


def half_of(w_ref, half):
    return jnp.concatenate(
        [
            w_ref[pl.ds(pl.multiple_of(2 * QUARTER * x + half * QUARTER, QUARTER), QUARTER), :]
            for x in range(X_CHIPS)
        ],
        axis=0,
    )


def cross_body(half_ref, dctx_ref, w_own_ref, w_other_ref, cross_ref):
    half = 1 - half_ref[0]
    dctx = dctx_ref[0:SLOTS, :]
    cross_ref[:, 0 : HALF // 2] = dot_cols(dctx, half_of(w_own_ref, half)).astype(BF16)
    cross_ref[:, HALF // 2 : HALF] = dot_cols(dctx, half_of(w_other_ref, half)).astype(BF16)


def spread_body(core_ref, half_ref, same_ref, cross_ref, w_own_ref, w_other_ref, line_ref, out_ref):
    core = core_ref[0]
    dctx = same_ref[0:SLOTS, :]
    parts = same_ref[SLOTS : SLOTS + 16, 0:SLOTS].astype(F32)
    places = (parts[0:1, :] * 16.0 + parts[1:2, :]).astype(I32)
    placed = one_hot(iota((FRAMES, SLOTS), 0) == places)
    shape = (HALF // 2, MODEL // 2)
    rows = jnp.zeros((SLOTS, MODEL // 2), F32)
    for side, (parity, w_ref) in enumerate(((core, w_own_ref), (1 - core, w_other_ref))):
        span = slice(HALF // 2 * side, HALF // 2 * (side + 1))
        drows = (dot_cols(dctx, half_of(w_ref, half_ref[0])) + cross_ref[:, span].astype(F32)).astype(BF16)
        q = iota(shape, 0)
        block = 2 * (X_CHIPS * ((q >> 5) & (Z_CHIPS // 2 - 1)) + (q >> 7)) + parity
        unpad = one_hot((BLOCK * block + (q & 31) == iota(shape, 1)) & ((q & 31) < BLOCK))
        rows = rows + dot(drows, unpad)
    out_ref[...] = dot(placed, rows.astype(BF16)).astype(BF16)


def targets_body(targets_ref, own_ref, low_ref, high_ref, line_ref, sent_ref, got_ref, out_ref):
    tail = slice(FRAMES, FRAMES + 16)
    line = line_ref[0:1, :] + jnp.sum(
        low_ref[tail, :].astype(F32) + high_ref[tail, :].astype(F32), axis=0, keepdims=True
    )
    inv_tgt = 1.0 / jnp.sqrt(
        sent_ref[SLOTS : SLOTS + 16, :] + got_ref[SLOTS : SLOTS + 16, :] + epsilon
    )
    for t in range(FRAMES // LANES):
        span = slice(LANES * t, LANES * (t + 1))
        scale = inv_tgt[TILES // 3 + t : TILES // 3 + t + 1, :]
        shift = line[:, span] * scale * scale * scale
        scale = jnp.broadcast_to(scale, (LANES, LANES)).T[:, 0:1]
        shift = jnp.broadcast_to(shift, (LANES, LANES)).T[:, 0:1]
        dtgt = own_ref[span, :] + low_ref[span, :].astype(F32) + high_ref[span, :].astype(F32)
        out_ref[span, :] = (dtgt * scale - targets_ref[span, :].astype(F32) * shift).astype(BF16)


def local(hidden, targets, w_proj, mask_counts, mask_pos, negatives):
    shard = lax.axis_index("dp")
    core = (shard % 2).astype(I32).reshape(1)
    half = lax.axis_index("param").astype(I32).reshape(1)
    n_dp = lax.axis_size("dp")
    n_pipe = lax.axis_size("pipe")
    peers = [[2 * (X_CHIPS * z + x) + c for x in range(X_CHIPS) for z in range(Z_CHIPS)] for c in range(2)]
    in_x = [[2 * (X_CHIPS * z + x) + c for x in range(X_CHIPS)] for z in range(Z_CHIPS) for c in range(2)]
    in_z = [[2 * (X_CHIPS * z + x) + c for z in range(Z_CHIPS)] for x in range(X_CHIPS) for c in range(2)]
    swap = [(i, i ^ 1) for i in range(n_dp)]
    upward = [(i, i + 1) for i in range(n_dp - 1)]
    downward = [(i + 1, i) for i in range(n_dp - 1)]
    back = [(i, (i - 1) % n_pipe) for i in range(n_pipe)]
    back_across = [
        (2 * i + a, 2 * ((i - 1) % n_pipe) + 1 - a) for i in range(n_pipe) for a in range(2)
    ]

    (w_blocks,) = call(blocks_body, [((Z_CHIPS, PAD, FEATS), BF16)], 0, 1, bytes_accessed=10**5)(w_proj)
    w_blocks = lax.all_to_all(w_blocks, "dp", 0, 0, axis_index_groups=in_z, tiled=True)
    (w_blocks,) = call(
        copies_body, [((X_CHIPS, HALF // X_CHIPS, FEATS), BF16)], 0, 1, bytes_accessed=10**6
    )(w_blocks.reshape(HALF // X_CHIPS, FEATS))
    w_own = lax.all_to_all(w_blocks, "dp", 0, 0, axis_index_groups=in_x, tiled=True).reshape(HALF, FEATS)

    own_targets = targets[0]
    low = lax.ppermute(own_targets, "dp", upward)
    high = lax.ppermute(own_targets, "dp", downward)
    positions = mask_pos[0, 0] - shard * FRAMES

    frames = jnp.concatenate([mask_pos[0, 0][None, :], negatives[0, 0]], axis=0) - (shard - 1) * FRAMES
    frames = jnp.pad(frames, ((0, LANES - COLUMNS), (0, 0)), constant_values=-1)

    rows_own, rows_other, turned_own, turned_other = call(
        rows_body,
        [((SLOTS, HALF), BF16)] * 2 + [((HALF, SLOTS), BF16)] * 2,
        1, 2, scratch=[pltpu.VMEM((HALF, SLOTS), F32)], flops=2 * 10**9, bytes_accessed=4 * 10**6, vmem=16,
    )(core, positions[:, None], hidden[0])
    turned_got = lax.ppermute(turned_other, "dp", swap)

    packed, times, frames = call(
        index_body, [((SLOTS, WORDS * LANES), I32), ((SLOTS, LANES), F32), ((SLOTS, LANES), I32)], 0, 1,
        scratch=[pltpu.VMEM((2 * WORDS + 2, LANES, SLOTS), I32)], flops=5 * 10**9, bytes_accessed=10**6,
    )(frames)

    window, norms = call(
        window_body, [((WINDOW, FEATS), BF16), ((16, LANES), F32)], 0, 3, flops=10**6, bytes_accessed=3 * 10**6
    )(low, own_targets, high)
    w_own, rows_own, rows_other, turned_own, turned_got, packed, times, frames, window, norms = lax.optimization_barrier(
        (w_own, rows_own, rows_other, turned_own, turned_got, packed, times, frames, window, norms)
    )
    w_other = lax.ppermute(w_own, "dp", swap)

    (part,) = call(
        part_body, [((SLOTS, FEATS), F32)], 0, 2, flops=3 * 10**8, bytes_accessed=2 * 10**6
    )(rows_own, w_own)
    sent, context = call(
        score_body, [((SLOTS + 16, LANES), F32), ((SLOTS, FEATS), F32)], 0, 6,
        scratch=[pltpu.VMEM((SLOTS, WINDOW), F32)], flops=10**9, bytes_accessed=6 * 10**6,
    )(part, rows_other, w_other, window, frames, norms)
    got = lax.ppermute(sent, "param", [(0, 1), (1, 0)])

    dctx, unit, pair = call(
        slots_body,
        [((SLOTS + 16, FEATS), BF16), ((SLOTS, FEATS), BF16), ((SLOTS, 2 * LANES), F32)],
        1, 8,
        scratch=[pltpu.VMEM((SLOTS, LANES), F32)] * 2 + [pltpu.VMEM((SLOTS, WINDOW), BF16)],
        flops=5 * 10**8, bytes_accessed=5 * 10**6,
    )(mask_counts[0], positions[None, :], sent, got, context, frames, times, packed, window)
    dctx_got = lax.ppermute(dctx, "dp", swap)

    (cross,) = call(
        cross_body, [((SLOTS, HALF), BF16)], 1, 3, flops=5 * 10**8, bytes_accessed=2 * 10**6
    )(half, dctx, w_own, w_other)
    cross, dctx_got = lax.optimization_barrier((cross, dctx_got))
    cross = lax.ppermute(cross, ("pipe", "param"), back_across)
    (share,) = call(
        share_body, [((HALF, FEATS), BF16)], 0, 4, flops=5 * 10**8, bytes_accessed=3 * 10**6
    )(turned_own, turned_got, dctx, dctx_got)
    pair, share, dctx = lax.optimization_barrier((pair, share, dctx))
    same = lax.ppermute(dctx, "pipe", back)
    shares = lax.all_to_all(
        share.reshape(X_CHIPS, HALF // X_CHIPS, FEATS), "dp", 0, 0, axis_index_groups=in_x, tiled=True
    )
    to_low, dtgt, to_high, line = call(
        frames_body,
        [((FRAMES + 16, FEATS), BF16), ((FRAMES, FEATS), F32), ((FRAMES + 16, FEATS), BF16), ((8, FRAMES), F32)],
        0, 3,
        scratch=[pltpu.VMEM((SLOTS, WINDOW), BF16), pltpu.VMEM((8, WINDOW), F32)],
        flops=10**5, bytes_accessed=10**4,
    )(pair, packed, unit)
    shares, line = lax.optimization_barrier((shares, line))
    (share,) = call(
        merge_body, [((HALF // X_CHIPS, FEATS), BF16)], 0, 1, flops=10**6, bytes_accessed=10**6
    )(shares)
    shares = lax.all_to_all(
        share.reshape(Z_CHIPS, PAD, FEATS), "dp", 0, 0, axis_index_groups=in_z, tiled=True
    )
    from_low = lax.ppermute(to_high, "dp", upward)
    from_high = lax.ppermute(to_low, "dp", downward)


    (token,) = call(
        token_body, [((8, LANES), F32)], 0, 0, flops=15 * 10**9, bytes_accessed=10**5, n_far=2
    )(cross, same)
    (copies,) = call(
        total_body, [((n_pipe, PAD, FEATS), F32)], 0, 1, flops=10**6, bytes_accessed=10**6, n_far=1
    )(shares, token)

    copies, line = lax.optimization_barrier((copies, line))
    pipe_parts = lax.all_to_all(copies, "pipe", 0, 0, tiled=True)
    (upstream,) = call(
        spread_body, [((FRAMES, MODEL // 2), BF16)], 2, 5,
        flops=1 * 10**9, bytes_accessed=4 * 10**6, vmem=16,
    )(core, half, same, cross, w_own, w_other, line)
    (grad_t,) = call(
        targets_body, [((FRAMES, FEATS), BF16)], 0, 7, flops=10**7, bytes_accessed=3 * 10**6
    )(own_targets, dtgt, from_low, from_high, line, sent, got)
    (grad_w,) = call(sum_body, [((BLOCK, FEATS), F32)], 0, 1, flops=10**5, bytes_accessed=10**5)(pipe_parts)
    return (grad_w, upstream[None], grad_t[None])


def solution(mesh):
    return jax.shard_map(
        local,
        mesh=mesh,
        in_specs=(
            P("pipe", "dp", None),
            P("pipe", "dp", "param"),
            P("dp", "param"),
            P("pipe", "dp"),
            P("pipe", "dp", None),
            P("pipe", "dp", None, None),
        ),
        out_specs=(P("dp", "param"), P("pipe", "dp", "param"), P("pipe", "dp", "param")),
        check_vma=False,
    )
```
